512 devices in a mesh: mem: 8 (over x, z_hi), col: 64 (over z_lo, y, core).
Axes of the slice: x: 4, y: 8, z: 8 (z_hi: 2, z_lo: 4; z = z_hi * 4 + z_lo), core: 2. Of those that a mesh axis runs over, the one named last changes fastest.
Arguments:
- perturbations: bfloat16 [8, 64, 384, 768], P('mem', None, 'col'), may hold values from -6 to 6
- gradient: float32 [64, 384, 768], P(None, 'col'), may hold values from -6 to 6
- member_weights: float32 [8], P('mem'), may hold values from 0.5 to 2
- scale_weights: float32 [3], replicated, may hold values from 0.2 to 2
- lon_filter: bfloat16 [3, 768, 768], P(None, 'mem'), may hold values from -1 to 1.5
- lat_filter: bfloat16 [3, 384, 384], P(None, 'col'), may hold values from -1 to 1.5
Outputs:
- increment: float32 [64, 384, 768], P('mem', 'col')
The draws below stay inside these ranges and needn't reach their ends.
All inputs are finite; a program needn't handle non-finite values.
Results may differ from the reference program's by a relative error of at most 0.01.
Values may be sent and summed in bfloat16 or wider, within the bound.
No kernel may reach another device: no remote copies, remote signals or barrier semaphores. Data moves between devices by JAX's collectives and lax.ppermute only.
A program may use at most 64 MiB of HBM per device.

```python
import math
import jax
import jax.numpy as jnp
from jax import lax

NLON = 768
NLAT = 384
SCALES = 3
NLEV = 64
MEMBERS = 8


def banded(key, count, periodic):
    places = jnp.arange(count, dtype=jnp.float32)
    spacing = jnp.abs(places[:, None] - places[None, :])
    if periodic:
        spacing = jnp.minimum(spacing, count - spacing)
    lengths = [max(1.0, count / 96.0), count / 24.0, count / 6.0]
    filters = []
    for scale_index in range(3):
        key_shape, key_jitter = jax.random.split(jax.random.fold_in(key, 17 + scale_index))
        ratio = spacing / lengths[scale_index]
        kernel = jnp.exp(-0.5 * ratio * ratio)
        kernel = kernel * jax.random.uniform(key_shape, (count, count), jnp.float32, 0.5, 1.5)
        kernel = kernel / jnp.sum(kernel, axis=1, keepdims=True)
        spread = 0.5
        jitter = jnp.clip(jax.random.normal(key_jitter, (count, count), jnp.float32), -4.0, 4.0)
        filters.append(kernel + jitter * spread / jnp.sqrt(count * 1.0))
    return jnp.stack(filters).astype(jnp.bfloat16)


def draw_lon_filter(key, part):
    return banded(key, NLON, True)


def draw_lat_filter(key, part):
    return banded(key, NLAT, False)


def steps_of(rng, extent, cuts, smallest, high):
    factor_of, own = 1.0, jax.random.fold_in(rng, 6)
    for axis_at, parts in cuts:
        heights = jnp.exp(jax.random.uniform(jax.random.fold_in(own, axis_at), (parts,), jnp.float32, smallest / len(cuts), high / len(cuts)))
        factor_of = factor_of * jnp.repeat(heights, extent[axis_at] // parts).reshape([-1 if axis == axis_at else 1 for axis in range(len(extent))])
    return factor_of


def bell_draw(own_key, extent, deviation, most, shards=(), kind=jnp.bfloat16):
    loudness = steps_of(own_key, extent, shards, -0.22, 0.18) if shards else 1.0
    values = jax.random.normal(own_key, extent, jnp.float32) * deviation * loudness
    return jnp.minimum(jnp.maximum(values, -most), most).astype(kind)


def setup_inputs(seed: int = 0) -> dict:
    splits = jax.random.split(jax.random.key(seed), 7)
    return {
        "perturbations": bell_draw(splits[0], (MEMBERS, NLEV, NLAT, NLON), 1.0, 6.0, ((0, 8), (2, 64))),
        "gradient": bell_draw(splits[1], (NLEV, NLAT, NLON), 1.0, 6.0, ((1, 64),), jnp.float32),
        "member_weights": jnp.clip(jnp.exp(math.log(2.0) - 1.3862944 * jax.random.uniform(splits[2], (MEMBERS,), jnp.float32) ** steps_of(splits[2], (MEMBERS,), ((0, 8),), -0.2, 0.2)), 0.5, 2.0),
        "scale_weights": jnp.clip(jnp.exp(jax.random.uniform(splits[3], (SCALES,), jnp.float32, math.log(0.2), math.log(2.0))), 0.2, 2.0),
        "lon_filter": draw_lon_filter(jax.random.fold_in(splits[6], 71), 0),
        "lat_filter": draw_lat_filter(jax.random.fold_in(splits[6], 71), 0),
    }


def reference(perturbations, gradient, member_weights, scale_weights, lon_filter, lat_filter):
    lon_full = lon_filter.astype(jnp.float32)
    lat_full = lat_filter.astype(jnp.float32)

    def one_member(total, inputs):
        member, weight = inputs
        member_full = member.astype(jnp.float32)
        schur = (member_full * gradient).astype(jnp.bfloat16)
        along = jnp.einsum('laj,sij->lsai', schur.astype(jnp.float32), lon_full).astype(jnp.bfloat16)
        across = jnp.einsum('sab,lsbi->lsai', lat_full, along.astype(jnp.float32))
        filtered = jnp.einsum('s,lsai->lai', scale_weights, across).astype(jnp.bfloat16)
        return total + weight * member_full * filtered.astype(jnp.float32), None

    start = jnp.zeros(gradient.shape, jnp.float32)
    total, unused = lax.scan(one_member, start, (perturbations, member_weights))
    return total
```

```python
import jax
import jax.numpy as jnp
from jax import lax
from jax.experimental import pallas as pl
from jax.experimental.pallas import tpu as pltpu
from jax.sharding import Mesh, PartitionSpec as P

MEM = ("x", "zh")
COL = ("zl", "y", "c")
SWAP = [(0, 1), (1, 0)]
F32, BF16 = jnp.float32, jnp.bfloat16


def filter_kernel(core, scale, field, lat, mine, other, out, lon, mid, sems):
    at = core[0]
    copies = []
    for x in range(4):
        for half, source in ((at, mine), (1 - at, other)):
            rows = pl.ds(pl.multiple_of((2 * x + half) * 96, 32), 96)
            copy = pltpu.make_async_copy(source.at[x], lon.at[:, rows, :], sems.at[len(copies)])
            copy.start()
            copies.append(copy)
    for s in range(3):
        across = jnp.dot(lat[s], field[...], preferred_element_type=F32)
        mid[s] = (scale[s] * across).astype(BF16)
    for copy in copies:
        copy.wait()
    total = jnp.zeros(out.shape, F32)
    for s in range(3):
        total += lax.dot_general(
            mid[s], lon[s], (((1,), (1,)), ((), ())), preferred_element_type=F32
        )
    out[...] = total.astype(BF16)


def filter_pair(core, scale, field, lat, mine, other):
    vmem = pl.BlockSpec(memory_space=pltpu.VMEM)
    smem = pl.BlockSpec(memory_space=pltpu.SMEM)
    hbm = pl.BlockSpec(memory_space=pl.ANY)
    return pl.pallas_call(
        filter_kernel,
        out_shape=jax.ShapeDtypeStruct((384, 768), BF16),
        in_specs=[smem, smem, vmem, vmem, hbm, hbm],
        out_specs=vmem,
        scratch_shapes=[
            pltpu.VMEM((3, 768, 768), BF16),
            pltpu.VMEM((3, 384, 768), BF16),
            pltpu.SemaphoreType.DMA((8,)),
        ],
        compiler_params=pltpu.CompilerParams(vmem_limit_bytes=40 * 2**20),
        cost_estimate=pl.CostEstimate(flops=2 * 10**9, bytes_accessed=5 * 10**6, transcendentals=0),
    )(core, scale, field, lat, mine, other)


def on_device(perturbations, gradient, member_weights, scale_weights, lon_filter, lat_filter):
    core = lax.axis_index("c")
    member = lax.axis_index(MEM)
    block = lax.ppermute(lon_filter, ("zh", "c"), [(0, 0), (1, 2), (2, 1), (3, 3)])
    mine = lax.all_gather(block, "x", axis=0)
    other = lax.ppermute(mine, "c", SWAP)
    turn = [(4 * x + z, 4 * z + x) for x in range(4) for z in range(4)]
    rows = jnp.pad(lat_filter.reshape(18, 384), ((0, 14), (0, 0)))
    rows = lax.ppermute(rows, ("x", "zl"), turn)
    rows = lax.all_gather(rows, "y", axis=0)
    rows = lax.all_gather(rows, "x", axis=0)
    swapped = lax.ppermute(rows, "c", SWAP)
    first = jnp.where(core == 0, rows, swapped)
    second = jnp.where(core == 0, swapped, rows)
    lat = jnp.stack([first, second], axis=2)[:, :, :, :18, :].reshape(64, 3, 6, 384)
    lat = lat.transpose(1, 0, 2, 3).reshape(3, 384, 384)
    weights = lax.all_gather(member_weights, MEM, axis=0, tiled=True)

    own = lax.all_to_all(perturbations[0].transpose(1, 0, 2), MEM, split_axis=1, concat_axis=1, tiled=True)
    level = lax.dynamic_slice_in_dim(gradient.transpose(1, 0, 2), member * 8, 8, axis=1)
    own = own.reshape(6, 8, 8, 768).astype(F32)
    schur = (own * level[:, None]).astype(BF16)
    schur = schur.transpose(1, 2, 0, 3).reshape(64, 2, 2304)
    field = lax.all_to_all(schur, COL, split_axis=0, concat_axis=0, tiled=True).reshape(384, 768)
    filtered = filter_pair(core.reshape(1).astype(jnp.int32), scale_weights, field, lat, mine, other)
    back = lax.all_to_all(filtered.reshape(64, 2, 2304), COL, split_axis=0, concat_axis=0, tiled=True)
    back = back.reshape(8, 8, 6, 768).transpose(2, 0, 1, 3).astype(F32)
    total = jnp.sum(weights[None, :, None, None] * own * back, axis=1)
    return total.transpose(1, 0, 2)


def solution(mesh):
    fine = Mesh(mesh.devices.reshape(4, 2, 4, 8, 2), MEM + COL)
    placed = (
        P(MEM, None, COL, None),
        P(None, COL, None),
        P(MEM),
        P(),
        P(None, MEM, None),
        P(None, COL, None),
    )
    return jax.shard_map(
        on_device, mesh=fine, in_specs=placed, out_specs=P(MEM, COL, None), check_vma=False
    )
```

```python
import jax
import jax.numpy as jnp
from jax import lax
from jax.experimental import pallas as pl
from jax.experimental.pallas import tpu as pltpu
from jax.sharding import Mesh, PartitionSpec as P

MEM = ("x", "zh")
COL = ("zl", "y", "c")
SWAP = [(0, 1), (1, 0)]
F32, BF16 = jnp.float32, jnp.bfloat16


VMEM = pl.BlockSpec(memory_space=pltpu.VMEM)
SMEM = pl.BlockSpec(memory_space=pltpu.SMEM)
ANY = pl.BlockSpec(memory_space=pl.ANY)
PLACES = ((0, 0, 48, 0), (1, 0, 48, 384), (2, 0, 32, 0), (2, 32, 16, 384))
STARTS = (288, 288, 336, 336)


def pack_kernel(y, block, *rest):
    pieces, (out, tiles, sem) = rest[:8], rest[8:]
    copy = pltpu.make_async_copy(block, out.at[pl.ds(0, 288)], sem)
    copy.start()
    for d, piece in enumerate(pieces):
        tiles[lax.rem(y[0] + 8 - d, 8)] = piece[...].astype(F32)
    for s, first, rows, column in PLACES:
        start = STARTS[PLACES.index((s, first, rows, column))]
        whole = jnp.concatenate([tiles[n, s, :6, :] for n in range(8)], axis=0)
        out[pl.ds(start, rows), pl.ds(column, 384)] = whole[first : first + rows].astype(BF16)
    out[pl.ds(352, 16), pl.ds(384, 384)] = jnp.zeros((16, 384), BF16)
    copy.wait()


def pack(y, block, pieces):
    return pl.pallas_call(
        pack_kernel,
        out_shape=jax.ShapeDtypeStruct((368, 768), BF16),
        in_specs=[SMEM, ANY] + [VMEM] * 8,
        out_specs=VMEM,
        scratch_shapes=[pltpu.VMEM((8, 3, 8, 384), F32), pltpu.SemaphoreType.DMA],
        cost_estimate=pl.CostEstimate(flops=10**6, bytes_accessed=2 * 10**6, transcendentals=0),
    )(y, block, *pieces)


def filter_kernel(place, scale, member, field, *rest):
    blocks, (out, lon, lat, mid, lon_sems, lat_sems) = rest[:8], rest[8:]
    lon_copies, lat_copies = [], []
    for n, block in enumerate(blocks):
        for m, ((s, first, rows, column), start) in enumerate(zip(PLACES, STARTS)):
            to = pl.ds(pl.multiple_of(place[1, n] * 48 + first, 16), rows)
            copy = pltpu.make_async_copy(
                block.at[pl.ds(start, rows), pl.ds(column, 384)], lat.at[s, to, :], lat_sems.at[n, m]
            )
            copy.start()
            lat_copies.append(copy)
    for n, block in enumerate(blocks):
        for s in range(3):
            to = pl.ds(pl.multiple_of(place[0, n] * 96, 32), 96)
            copy = pltpu.make_async_copy(
                block.at[pl.ds(96 * s, 96), :], lon.at[s, to, :], lon_sems.at[n, s]
            )
            copy.start()
            lon_copies.append(copy)
    for copy in lat_copies:
        copy.wait()
    for s in range(3):
        across = jnp.dot(lat[s], field[...], preferred_element_type=F32)
        mid[s] = (scale[s] * member[0] * across).astype(BF16)
    for copy in lon_copies:
        copy.wait()
    total = jnp.zeros(out.shape, F32)
    for s in range(3):
        total += lax.dot_general(
            mid[s], lon[s], (((1,), (1,)), ((), ())), preferred_element_type=F32
        )
    out[...] = total.astype(BF16)


def filter_pair(place, scale, member, field, blocks):
    return pl.pallas_call(
        filter_kernel,
        out_shape=jax.ShapeDtypeStruct((384, 768), BF16),
        in_specs=[SMEM, SMEM, SMEM, VMEM] + [ANY] * 8,
        out_specs=VMEM,
        scratch_shapes=[
            pltpu.VMEM((3, 768, 768), BF16),
            pltpu.VMEM((3, 384, 384), BF16),
            pltpu.VMEM((3, 384, 768), BF16),
            pltpu.SemaphoreType.DMA((8, 3)),
            pltpu.SemaphoreType.DMA((8, 4)),
        ],
        compiler_params=pltpu.CompilerParams(vmem_limit_bytes=40 * 2**20),
        cost_estimate=pl.CostEstimate(flops=2 * 10**9, bytes_accessed=5 * 10**6, transcendentals=0),
    )(place, scale, member, field, *blocks)


def on_device(perturbations, gradient, member_weights, scale_weights, lon_filter, lat_filter):
    x, y, core = lax.axis_index("x"), lax.axis_index("y"), lax.axis_index("c")
    block = lax.ppermute(lon_filter, ("zh", "c"), [(0, 0), (1, 2), (2, 1), (3, 3)])
    own = perturbations[0].transpose(1, 0, 2).reshape(6, 8, 8, 768).transpose(1, 0, 2, 3)
    own = lax.all_to_all(own, MEM, split_axis=0, concat_axis=0, tiled=True)
    rows = jnp.pad(lat_filter, ((0, 0), (0, 2), (0, 0)))
    pieces = [
        lax.ppermute(rows, ("x", "zl", "y"), [
            (32 * a + 8 * b + r, 32 * b + 8 * a + (r + d) % 8)
            for a in range(4) for b in range(4) for r in range(8)
        ])
        for d in range(8)
    ]
    turn = [((c // 8) * 64 + m * 8 + c % 8, m * 64 + c) for m in range(8) for c in range(64)]
    weight = lax.ppermute(member_weights, MEM + COL, turn)
    own, block, pieces, weight = lax.optimization_barrier((own, block, pieces, weight))

    packed = pack(y.reshape(1).astype(jnp.int32), block.reshape(288, 768), pieces)
    own, packed = lax.optimization_barrier((own, packed))
    mine = [packed] + [
        lax.ppermute(packed, "x", [(i, (i + d) % 4) for i in range(4)]) for d in (1, 3, 2)
    ]
    blocks = mine + [lax.ppermute(b, "c", SWAP) for b in mine]
    froms = jnp.stack([(x + 4 - d) % 4 for d in (0, 1, 3, 2)]).astype(jnp.int32)
    place = jnp.concatenate([2 * froms + core, 2 * froms + 1 - core]).astype(jnp.int32)
    place = jnp.stack([place, place])

    member = lax.axis_index(MEM)
    level = lax.dynamic_slice_in_dim(gradient.transpose(1, 0, 2), member * 8, 8, axis=1)
    own = own.astype(F32)
    schur = (own * level[None]).astype(BF16)
    schur = schur.transpose(0, 2, 1, 3).reshape(64, 2, 2304)
    field = lax.all_to_all(schur, COL, split_axis=0, concat_axis=0, tiled=True).reshape(384, 768)
    filtered = filter_pair(place, scale_weights, weight, field, blocks).reshape(64, 2, 2304)
    back = lax.all_to_all(filtered, ("zl", "c", "y"), split_axis=0, concat_axis=0, tiled=True)
    back = back.reshape(4, 2, 2, 4, 6, 768).transpose(0, 2, 4, 3, 1, 5).reshape(8, 6, 8, 768)
    return jnp.sum(own * back.astype(F32), axis=0).transpose(1, 0, 2)


def solution(mesh):
    fine = Mesh(mesh.devices.reshape(4, 2, 4, 8, 2), MEM + COL)
    placed = (
        P(MEM, None, COL, None),
        P(None, COL, None),
        P(MEM),
        P(),
        P(None, MEM, None),
        P(None, COL, None),
    )
    return jax.shard_map(
        on_device, mesh=fine, in_specs=placed, out_specs=P(MEM, COL, None), check_vma=False
    )
```

```python
import jax
import jax.numpy as jnp
from jax import lax
from jax.experimental import pallas as pl
from jax.experimental.pallas import tpu as pltpu
from jax.sharding import Mesh, PartitionSpec as P

MEM = ("x", "zh")
COL = ("zl", "y", "c")
SWAP = [(0, 1), (1, 0)]
F32, BF16 = jnp.float32, jnp.bfloat16


VMEM = pl.BlockSpec(memory_space=pltpu.VMEM)
SMEM = pl.BlockSpec(memory_space=pltpu.SMEM)
ANY = pl.BlockSpec(memory_space=pl.ANY)
PLACES = ((288, 0, 48, 0, 0), (288, 384, 48, 1, 0), (336, 0, 32, 2, 0), (336, 384, 16, 2, 32))


def pack_kernel(block, tiles, out, sem):
    copy = pltpu.make_async_copy(block, out.at[pl.ds(0, 288)], sem)
    copy.start()
    for row, column, rows, s, first in PLACES:
        whole = jnp.concatenate([tiles[n, s, :6, :].astype(F32) for n in range(8)], axis=0)
        out[pl.ds(row, rows), pl.ds(column, 384)] = whole[first : first + rows].astype(BF16)
    out[pl.ds(352, 16), pl.ds(384, 384)] = jnp.zeros((16, 384), BF16)
    copy.wait()


def pack(block, tiles):
    return pl.pallas_call(
        pack_kernel,
        out_shape=jax.ShapeDtypeStruct((368, 768), BF16),
        in_specs=[ANY, VMEM],
        out_specs=VMEM,
        scratch_shapes=[pltpu.SemaphoreType.DMA],
        cost_estimate=pl.CostEstimate(flops=10**6, bytes_accessed=2 * 10**6, transcendentals=0),
    )(block, tiles)


def filter_kernel(core, scale, member, field, mine, other, out, lon, lat, mid, lon_sems, lat_sems):
    lon_copies, lat_copies = [], []
    for n in range(8):
        x, part, half = n % 4, (mine, other)[n // 4], (core[0], 1 - core[0])[n // 4]
        for m, (row, column, rows, s, first) in enumerate(PLACES):
            to = pl.ds(pl.multiple_of((2 * x + half) * 48 + first, 16), rows)
            copy = pltpu.make_async_copy(
                part.at[x, pl.ds(row, rows), pl.ds(column, 384)], lat.at[s, to, :], lat_sems.at[n, m]
            )
            copy.start()
            lat_copies.append(copy)
    for n in range(8):
        x, part, half = n % 4, (mine, other)[n // 4], (core[0], 1 - core[0])[n // 4]
        for s in range(3):
            to = pl.ds(pl.multiple_of((2 * x + half) * 96, 32), 96)
            copy = pltpu.make_async_copy(
                part.at[x, pl.ds(96 * s, 96), :], lon.at[s, to, :], lon_sems.at[n, s]
            )
            copy.start()
            lon_copies.append(copy)
    for copy in lat_copies:
        copy.wait()
    for s in range(3):
        across = jnp.dot(lat[s], field[...], preferred_element_type=F32)
        mid[s] = (scale[s] * member[0] * across).astype(BF16)
    for copy in lon_copies:
        copy.wait()
    total = jnp.zeros(out.shape, F32)
    for s in range(3):
        total += lax.dot_general(
            mid[s], lon[s], (((1,), (1,)), ((), ())), preferred_element_type=F32
        )
    out[...] = total.astype(BF16)


def filter_pair(core, scale, member, field, mine, other):
    return pl.pallas_call(
        filter_kernel,
        out_shape=jax.ShapeDtypeStruct((384, 768), BF16),
        in_specs=[SMEM, SMEM, SMEM, VMEM, ANY, ANY],
        out_specs=VMEM,
        scratch_shapes=[
            pltpu.VMEM((3, 768, 768), BF16),
            pltpu.VMEM((3, 384, 384), BF16),
            pltpu.VMEM((3, 384, 768), BF16),
            pltpu.SemaphoreType.DMA((8, 3)),
            pltpu.SemaphoreType.DMA((8, 4)),
        ],
        compiler_params=pltpu.CompilerParams(vmem_limit_bytes=40 * 2**20),
        cost_estimate=pl.CostEstimate(flops=2 * 10**9, bytes_accessed=5 * 10**6, transcendentals=0),
    )(core, scale, member, field, mine, other)


def final_kernel(own, back, out):
    for r in range(6):
        total = jnp.zeros((8, 768), F32)
        for k in range(8):
            parts = [
                back[k // 2, l % 2, 4 * (k % 2) + l // 2, r, :].astype(F32).reshape(1, 768)
                for l in range(8)
            ]
            total += own[k, r].astype(F32) * jnp.concatenate(parts, axis=0)
        out[r] = total


def final_sum(own, back):
    return pl.pallas_call(
        final_kernel,
        out_shape=jax.ShapeDtypeStruct((6, 8, 768), F32),
        in_specs=[VMEM, VMEM],
        out_specs=VMEM,
        cost_estimate=pl.CostEstimate(flops=10**6, bytes_accessed=2 * 10**6, transcendentals=0),
    )(own, back)


def on_device(perturbations, gradient, member_weights, scale_weights, lon_filter, lat_filter):
    core = lax.axis_index("c")
    own = perturbations[0].transpose(1, 0, 2).reshape(6, 8, 8, 768).transpose(1, 0, 2, 3)
    own = lax.all_to_all(own, MEM, split_axis=0, concat_axis=0, tiled=True)
    block = lax.ppermute(lon_filter, ("zh", "c"), [(0, 0), (1, 2), (2, 1), (3, 3)])
    rows = jnp.pad(lat_filter, ((0, 0), (0, 2), (0, 0)))
    rows = lax.ppermute(rows, ("x", "zl"), [(4 * a + b, 4 * b + a) for a in range(4) for b in range(4)])
    tiles = jnp.broadcast_to(rows[None], (8, 3, 8, 384))
    tiles = lax.all_to_all(tiles, "y", split_axis=0, concat_axis=0, tiled=True)
    packed = pack(block.reshape(288, 768), tiles)
    mine = lax.all_gather(packed, "x", axis=0)
    member = lax.axis_index(MEM)
    level = lax.dynamic_slice_in_dim(gradient.transpose(1, 0, 2), member * 8, 8, axis=1)
    schur = (own.astype(F32) * level[None]).astype(BF16)
    schur = schur.transpose(0, 2, 1, 3).reshape(64, 2, 2304)
    turn = [((c // 8) * 64 + m * 8 + c % 8, m * 64 + c) for m in range(8) for c in range(64)]
    weight = lax.optimization_barrier((member_weights, schur))[0]
    weight = lax.ppermute(weight, MEM + COL, turn)
    mine = lax.optimization_barrier((mine, schur))[0]
    other = lax.ppermute(mine, "c", SWAP)
    field = lax.all_to_all(schur, COL, split_axis=0, concat_axis=0, tiled=True).reshape(384, 768)
    core = core.reshape(1).astype(jnp.int32)
    filtered = filter_pair(core, scale_weights, weight, field, mine, other).reshape(64, 2, 2304)
    back = lax.all_to_all(filtered, ("zl", "c", "y"), split_axis=0, concat_axis=0, tiled=True)
    return final_sum(own, back.reshape(4, 2, 8, 6, 768)).transpose(1, 0, 2)


def solution(mesh):
    fine = Mesh(mesh.devices.reshape(4, 2, 4, 8, 2), MEM + COL)
    placed = (
        P(MEM, None, COL, None),
        P(None, COL, None),
        P(MEM),
        P(),
        P(None, MEM, None),
        P(None, COL, None),
    )
    return jax.shard_map(
        on_device, mesh=fine, in_specs=placed, out_specs=P(MEM, COL, None), check_vma=False
    )
```

```python
import jax
import jax.numpy as jnp
from jax import lax
from jax.experimental import pallas as pl
from jax.experimental.pallas import tpu as pltpu
from jax.sharding import Mesh, PartitionSpec as P

MEM = ("x", "zh")
COL = ("zl", "y", "c")
SWAP = [(0, 1), (1, 0)]
F32, BF16 = jnp.float32, jnp.bfloat16


VMEM = pl.BlockSpec(memory_space=pltpu.VMEM)
SMEM = pl.BlockSpec(memory_space=pltpu.SMEM)
ANY = pl.BlockSpec(memory_space=pl.ANY)
HBM = pl.BlockSpec(memory_space=pltpu.MemorySpace.HBM)


def pack_kernel(block, tiles, out, sem):
    copy = pltpu.make_async_copy(block, out.at[pl.ds(0, 288)], sem)
    copy.start()
    for half in range(2):
        for part in range(4):
            first = 16 * half + 4 * part
            rows = [tiles[first + n, :6, :].astype(F32) for n in range(4)]
            out[pl.ds(288 + 24 * part, 24), pl.ds(384 * half, 384)] = jnp.concatenate(rows, axis=0).astype(BF16)
    copy.wait()


def pack(block, tiles):
    return pl.pallas_call(
        pack_kernel,
        out_shape=jax.ShapeDtypeStruct((384, 768), BF16),
        in_specs=[ANY, VMEM],
        out_specs=VMEM,
        scratch_shapes=[pltpu.SemaphoreType.DMA],
        cost_estimate=pl.CostEstimate(flops=10**6, bytes_accessed=2 * 10**6, transcendentals=0),
    )(block, tiles)


def filter_kernel(core, scale, member, field, mine, other, out, lon, lat, mid, lon_sems, lat_sems):
    lon_copies, lat_copies = [], []
    sides = ((mine, core[0]), (other, 1 - core[0]))
    for m, (part, half) in enumerate(sides):
        for s in range(3):
            for h in range(2):
                to = pl.ds(pl.multiple_of(half * 192 + 96 * h, 32), 96)
                copy = pltpu.make_async_copy(
                    part.at[s, pl.ds(288, 96), pl.ds(384 * h, 384)], lat.at[s, to, :], lat_sems.at[m, s, h]
                )
                copy.start()
                lat_copies.append(copy)
    for s in range(3):
        for m, (part, half) in enumerate(sides):
            for x in range(4):
                to = pl.ds(pl.multiple_of((2 * x + half) * 96, 32), 96)
                copy = pltpu.make_async_copy(
                    part.at[x, pl.ds(96 * s, 96), :], lon.at[s, to, :], lon_sems.at[m, s, x]
                )
                copy.start()
                lon_copies.append(copy)
    for copy in lat_copies:
        copy.wait()
    for s in range(3):
        across = jnp.dot(lat[s], field[...], preferred_element_type=F32)
        mid[s] = (scale[s] * member[0] * across).astype(BF16)
    for copy in lon_copies:
        copy.wait()
    total = jnp.zeros(out.shape, F32)
    for s in range(3):
        total += lax.dot_general(
            mid[s], lon[s], (((1,), (1,)), ((), ())), preferred_element_type=F32
        )
    out[...] = total.astype(BF16)


def filter_pair(core, scale, member, field, mine, other):
    return pl.pallas_call(
        filter_kernel,
        out_shape=jax.ShapeDtypeStruct((384, 768), BF16),
        in_specs=[SMEM, SMEM, SMEM, VMEM, HBM, HBM],
        out_specs=VMEM,
        scratch_shapes=[
            pltpu.VMEM((3, 768, 768), BF16),
            pltpu.VMEM((3, 384, 384), BF16),
            pltpu.VMEM((3, 384, 768), BF16),
            pltpu.SemaphoreType.DMA((2, 3, 4)),
            pltpu.SemaphoreType.DMA((2, 3, 2)),
        ],
        compiler_params=pltpu.CompilerParams(vmem_limit_bytes=62 * 2**20),
        cost_estimate=pl.CostEstimate(flops=2 * 10**9, bytes_accessed=5 * 10**6, transcendentals=0),
    )(core, scale, member, field, mine, other)


def final_kernel(own, back, out):
    for r in range(6):
        total = jnp.zeros((8, 768), F32)
        for k in range(8):
            parts = [
                back[l % 2, k // 2, 4 * (k % 2) + l // 2, r, :].astype(F32).reshape(1, 768)
                for l in range(8)
            ]
            total += own[k, r].astype(F32) * jnp.concatenate(parts, axis=0)
        out[r] = total


def final_sum(own, back):
    return pl.pallas_call(
        final_kernel,
        out_shape=jax.ShapeDtypeStruct((6, 8, 768), F32),
        in_specs=[VMEM, VMEM],
        out_specs=VMEM,
        cost_estimate=pl.CostEstimate(flops=10**6, bytes_accessed=2 * 10**6, transcendentals=0),
    )(own, back)


def on_device(perturbations, gradient, member_weights, scale_weights, lon_filter, lat_filter):
    core = lax.axis_index("c")
    own = perturbations[0].transpose(1, 0, 2).reshape(6, 8, 8, 768).transpose(1, 0, 2, 3)
    own = lax.all_to_all(own, MEM, split_axis=0, concat_axis=0, tiled=True)
    block = lax.ppermute(lon_filter, ("zh", "c"), [(0, 0), (1, 2), (2, 1), (3, 3)])
    rows = lax.dynamic_index_in_dim(lat_filter, jnp.minimum(lax.axis_index("x"), 2), 0, False)
    tiles = jnp.broadcast_to(jnp.pad(rows, ((0, 2), (0, 0)))[None], (32, 8, 384))
    tiles = lax.all_to_all(tiles, ("zl", "y"), split_axis=0, concat_axis=0, tiled=True)
    packed = pack(block.reshape(288, 768), tiles)
    mine = lax.all_gather(packed, "x", axis=0)
    turn = [((c // 8) * 64 + m * 8 + c % 8, m * 64 + c) for m in range(8) for c in range(64)]
    weight = lax.ppermute(member_weights, MEM + COL, turn)
    own, weight = lax.optimization_barrier((own, weight))

    member = lax.axis_index(MEM)
    level = lax.dynamic_slice_in_dim(gradient.transpose(1, 0, 2), member * 8, 8, axis=1)
    schur = (own.astype(F32) * level[None]).astype(BF16)
    schur = schur.transpose(0, 2, 1, 3).reshape(64, 2, 2304)
    field = lax.all_to_all(schur, COL, split_axis=0, concat_axis=0, tiled=True).reshape(384, 768)
    mine = lax.optimization_barrier((mine, field))[0]
    other = lax.ppermute(mine, "c", SWAP)
    core = core.reshape(1).astype(jnp.int32)
    filtered = filter_pair(core, scale_weights, weight, field, mine, other).reshape(64, 2, 2304)
    back = lax.all_to_all(filtered, ("c", "zl", "y"), split_axis=0, concat_axis=0, tiled=True)
    return final_sum(own, back.reshape(2, 4, 8, 6, 768)).transpose(1, 0, 2)


def solution(mesh):
    fine = Mesh(mesh.devices.reshape(4, 2, 4, 8, 2), MEM + COL)
    placed = (
        P(MEM, None, COL, None),
        P(None, COL, None),
        P(MEM),
        P(),
        P(None, MEM, None),
        P(None, COL, None),
    )
    return jax.shard_map(
        on_device, mesh=fine, in_specs=placed, out_specs=P(MEM, COL, None), check_vma=False
    )
```

```python
import jax
import jax.numpy as jnp
from jax import lax
from jax.experimental import pallas as pl
from jax.experimental.pallas import tpu as pltpu
from jax.sharding import Mesh, PartitionSpec as P

MEM = ("x", "zh")
COL = ("zl", "y", "c")
SWAP = [(0, 1), (1, 0)]
F32, BF16 = jnp.float32, jnp.bfloat16


VMEM = pl.BlockSpec(memory_space=pltpu.VMEM)
SMEM = pl.BlockSpec(memory_space=pltpu.SMEM)
ANY = pl.BlockSpec(memory_space=pl.ANY)
HBM = pl.BlockSpec(memory_space=pltpu.MemorySpace.HBM)


def pack_kernel(block, tiles, out):
    out[pl.ds(0, 288), :] = block[...]
    for half in range(2):
        for part in range(4):
            first = 16 * half + 4 * part
            rows = [tiles[first + n, :6, :].astype(F32) for n in range(4)]
            out[pl.ds(288 + 24 * part, 24), pl.ds(384 * half, 384)] = jnp.concatenate(rows, axis=0).astype(BF16)


def pack(block, tiles):
    return pl.pallas_call(
        pack_kernel,
        out_shape=jax.ShapeDtypeStruct((384, 768), BF16),
        in_specs=[VMEM, VMEM],
        out_specs=VMEM,
        cost_estimate=pl.CostEstimate(flops=10**6, bytes_accessed=2 * 10**6, transcendentals=0),
    )(block, tiles)


def filter_kernel(core, scale, member, field, mine, *rest):
    others, (out, lon, lat, mid, lon_sems, lat_sems) = rest[:4], rest[4:]
    lon_copies, lat_copies = [], []
    sides = (([mine.at[x] for x in range(4)], core[0]), (others, 1 - core[0]))
    for m, (part, half) in enumerate(sides):
        for s in range(3):
            for h in range(2):
                to = pl.ds(pl.multiple_of(half * 192 + 96 * h, 32), 96)
                copy = pltpu.make_async_copy(
                    part[s].at[pl.ds(288, 96), pl.ds(384 * h, 384)], lat.at[s, to, :], lat_sems.at[m, s, h]
                )
                copy.start()
                lat_copies.append(copy)
    for s in range(3):
        for m, (part, half) in enumerate(sides):
            for x in range(4):
                to = pl.ds(pl.multiple_of((2 * x + half) * 96, 32), 96)
                copy = pltpu.make_async_copy(
                    part[x].at[pl.ds(96 * s, 96), :], lon.at[s, to, :], lon_sems.at[m, s, x]
                )
                copy.start()
                lon_copies.append(copy)
    for copy in lat_copies:
        copy.wait()
    for s in range(3):
        across = jnp.dot(lat[s], field[...], preferred_element_type=F32)
        mid[s] = (scale[s] * member[0] * across).astype(BF16)
    for copy in lon_copies:
        copy.wait()
    total = jnp.zeros(out.shape, F32)
    for s in range(3):
        total += lax.dot_general(
            mid[s], lon[s], (((1,), (1,)), ((), ())), preferred_element_type=F32
        )
    out[...] = total.astype(BF16)


def filter_pair(core, scale, member, field, mine, others):
    return pl.pallas_call(
        filter_kernel,
        out_shape=jax.ShapeDtypeStruct((384, 768), BF16),
        in_specs=[SMEM, SMEM, SMEM, VMEM] + [HBM] * 5,
        out_specs=VMEM,
        scratch_shapes=[
            pltpu.VMEM((3, 768, 768), BF16),
            pltpu.VMEM((3, 384, 384), BF16),
            pltpu.VMEM((3, 384, 768), BF16),
            pltpu.SemaphoreType.DMA((2, 3, 4)),
            pltpu.SemaphoreType.DMA((2, 3, 2)),
        ],
        compiler_params=pltpu.CompilerParams(vmem_limit_bytes=20 * 2**20),
        cost_estimate=pl.CostEstimate(flops=2 * 10**9, bytes_accessed=5 * 10**6, transcendentals=0),
    )(core, scale, member, field, mine, *others)


def final_kernel(own, back, out):
    for r in range(6):
        total = jnp.zeros((8, 768), F32)
        for k in range(8):
            parts = [
                back[l % 2, k // 2, 4 * (k % 2) + l // 2, r, :].astype(F32).reshape(1, 768)
                for l in range(8)
            ]
            total += own[k, r].astype(F32) * jnp.concatenate(parts, axis=0)
        out[r] = total


def final_sum(own, back):
    return pl.pallas_call(
        final_kernel,
        out_shape=jax.ShapeDtypeStruct((6, 8, 768), F32),
        in_specs=[VMEM, VMEM],
        out_specs=VMEM,
        cost_estimate=pl.CostEstimate(flops=10**6, bytes_accessed=2 * 10**6, transcendentals=0),
    )(own, back)


def on_device(perturbations, gradient, member_weights, scale_weights, lon_filter, lat_filter):
    core = lax.axis_index("c")
    own = perturbations[0].transpose(1, 0, 2).reshape(6, 8, 8, 768).transpose(1, 0, 2, 3)
    own = lax.all_to_all(own, MEM, split_axis=0, concat_axis=0, tiled=True)
    block = lax.ppermute(lon_filter, ("zh", "c"), [(0, 0), (1, 2), (2, 1), (3, 3)])
    rows = lax.dynamic_index_in_dim(lat_filter, jnp.minimum(lax.axis_index("x"), 2), 0, False)
    tiles = jnp.broadcast_to(jnp.pad(rows, ((0, 2), (0, 0)))[None], (32, 8, 384))
    tiles = lax.all_to_all(tiles, ("zl", "y"), split_axis=0, concat_axis=0, tiled=True)
    turn = [((c // 8) * 64 + m * 8 + c % 8, m * 64 + c) for m in range(8) for c in range(64)]
    weight = lax.ppermute(member_weights, MEM + COL, turn)
    block, weight = lax.optimization_barrier((block, weight))
    packed = pack(block.reshape(288, 768), tiles)
    mine = lax.all_gather(packed, "x", axis=0)
    member = lax.axis_index(MEM)
    level = lax.dynamic_slice_in_dim(gradient.transpose(1, 0, 2), member * 8, 8, axis=1)
    schur = (own.astype(F32) * level[None]).astype(BF16)
    schur = schur.transpose(0, 2, 1, 3).reshape(64, 2, 2304)
    field = lax.all_to_all(schur, COL, split_axis=0, concat_axis=0, tiled=True).reshape(384, 768)
    mine = lax.optimization_barrier((mine, schur))[0]
    others = [lax.ppermute(mine[n], "c", SWAP) for n in range(4)]
    core = core.reshape(1).astype(jnp.int32)
    filtered = filter_pair(core, scale_weights, weight, field, mine, others).reshape(64, 2, 2304)
    back = lax.all_to_all(filtered, ("c", "zl", "y"), split_axis=0, concat_axis=0, tiled=True)
    return final_sum(own, back.reshape(2, 4, 8, 6, 768)).transpose(1, 0, 2)


def solution(mesh):
    fine = Mesh(mesh.devices.reshape(4, 2, 4, 8, 2), MEM + COL)
    placed = (
        P(MEM, None, COL, None),
        P(None, COL, None),
        P(MEM),
        P(),
        P(None, MEM, None),
        P(None, COL, None),
    )
    return jax.shard_map(
        on_device, mesh=fine, in_specs=placed, out_specs=P(MEM, COL, None), check_vma=False
    )
```

```python
import jax
import jax.numpy as jnp
from jax import lax
from jax.experimental import pallas as pl
from jax.experimental.pallas import tpu as pltpu
from jax.sharding import Mesh, PartitionSpec as P

MEM = ("x", "zh")
COL = ("zl", "y", "c")
SWAP = [(0, 1), (1, 0)]
F32, BF16 = jnp.float32, jnp.bfloat16


VMEM = pl.BlockSpec(memory_space=pltpu.VMEM)
SMEM = pl.BlockSpec(memory_space=pltpu.SMEM)
ANY = pl.BlockSpec(memory_space=pl.ANY)
HBM = pl.BlockSpec(memory_space=pltpu.MemorySpace.HBM)


def pack_kernel(block, tiles, out):
    out[pl.ds(0, 288), :] = block[...]
    for half in range(2):
        for part in range(4):
            first = 16 * half + 4 * part
            rows = [tiles[first + n, :6, :].astype(F32) for n in range(4)]
            out[pl.ds(288 + 24 * part, 24), pl.ds(384 * half, 384)] = jnp.concatenate(rows, axis=0).astype(BF16)


def pack(block, tiles):
    return pl.pallas_call(
        pack_kernel,
        out_shape=jax.ShapeDtypeStruct((384, 768), BF16),
        in_specs=[VMEM, VMEM],
        out_specs=VMEM,
        cost_estimate=pl.CostEstimate(flops=10**6, bytes_accessed=2 * 10**6, transcendentals=0),
    )(block, tiles)


def filter_kernel(core, scale, member, field, mine, other, out, lon, lat, mid, lon_sems, lat_sems):
    lon_copies, lat_copies = [], []
    sides = ((mine, core[0]), (other, 1 - core[0]))
    for m, (part, half) in enumerate(sides):
        for s in range(3):
            for h in range(2):
                to = pl.ds(pl.multiple_of(half * 192 + 96 * h, 32), 96)
                copy = pltpu.make_async_copy(
                    part.at[s, pl.ds(288, 96), pl.ds(384 * h, 384)], lat.at[s, to, :], lat_sems.at[m, s, h]
                )
                copy.start()
                lat_copies.append(copy)
    for s in range(3):
        for m, (part, half) in enumerate(sides):
            for x in range(4):
                to = pl.ds(pl.multiple_of((2 * x + half) * 96, 32), 96)
                copy = pltpu.make_async_copy(
                    part.at[x, pl.ds(96 * s, 96), :], lon.at[s, to, :], lon_sems.at[m, s, x]
                )
                copy.start()
                lon_copies.append(copy)
    for copy in lat_copies:
        copy.wait()
    for s in range(3):
        across = jnp.dot(lat[s], field[...], preferred_element_type=F32)
        mid[s] = (scale[s] * member[0] * across).astype(BF16)
    for copy in lon_copies:
        copy.wait()
    total = jnp.zeros(out.shape, F32)
    for s in range(3):
        total += lax.dot_general(
            mid[s], lon[s], (((1,), (1,)), ((), ())), preferred_element_type=F32
        )
    out[...] = total.astype(BF16)


def filter_pair(core, scale, member, field, mine, other):
    return pl.pallas_call(
        filter_kernel,
        out_shape=jax.ShapeDtypeStruct((384, 768), BF16),
        in_specs=[SMEM, SMEM, SMEM, VMEM, HBM, HBM],
        out_specs=VMEM,
        scratch_shapes=[
            pltpu.VMEM((3, 768, 768), BF16),
            pltpu.VMEM((3, 384, 384), BF16),
            pltpu.VMEM((3, 384, 768), BF16),
            pltpu.SemaphoreType.DMA((2, 3, 4)),
            pltpu.SemaphoreType.DMA((2, 3, 2)),
        ],
        compiler_params=pltpu.CompilerParams(vmem_limit_bytes=40 * 2**20),
        cost_estimate=pl.CostEstimate(flops=2 * 10**9, bytes_accessed=5 * 10**6, transcendentals=0),
    )(core, scale, member, field, mine, other)


def final_kernel(own, back, out):
    for r in range(6):
        total = jnp.zeros((8, 768), F32)
        for k in range(8):
            parts = [
                back[l % 2, k // 2, 4 * (k % 2) + l // 2, r, :].astype(F32).reshape(1, 768)
                for l in range(8)
            ]
            total += own[k, r].astype(F32) * jnp.concatenate(parts, axis=0)
        out[r] = total


def final_sum(own, back):
    return pl.pallas_call(
        final_kernel,
        out_shape=jax.ShapeDtypeStruct((6, 8, 768), F32),
        in_specs=[VMEM, VMEM],
        out_specs=VMEM,
        cost_estimate=pl.CostEstimate(flops=10**6, bytes_accessed=2 * 10**6, transcendentals=0),
    )(own, back)


def on_device(perturbations, gradient, member_weights, scale_weights, lon_filter, lat_filter):
    core = lax.axis_index("c")
    own = perturbations[0].transpose(1, 0, 2).reshape(6, 8, 8, 768).transpose(1, 0, 2, 3)
    own = lax.all_to_all(own, MEM, split_axis=0, concat_axis=0, tiled=True)
    turn = [((c // 8) * 64 + m * 8 + c % 8, m * 64 + c) for m in range(8) for c in range(64)]
    weight = lax.ppermute(member_weights, MEM + COL, turn)
    block = lax.ppermute(lon_filter, ("zh", "c"), [(0, 0), (1, 2), (2, 1), (3, 3)])
    rows = lax.dynamic_index_in_dim(lat_filter, jnp.minimum(lax.axis_index("x"), 2), 0, False)
    tiles = jnp.broadcast_to(jnp.pad(rows, ((0, 2), (0, 0)))[None], (32, 8, 384))
    own, weight, block, tiles = lax.optimization_barrier((own, weight, block, tiles))
    tiles = lax.all_to_all(tiles, ("zl", "y"), split_axis=0, concat_axis=0, tiled=True)
    packed = pack(block.reshape(288, 768), tiles)
    own, packed = lax.optimization_barrier((own, packed))
    mine = lax.all_gather(packed, "x", axis=0)
    member = lax.axis_index(MEM)
    level = lax.dynamic_slice_in_dim(gradient.transpose(1, 0, 2), member * 8, 8, axis=1)
    schur = (own.astype(F32) * level[None]).astype(BF16)
    schur = schur.transpose(0, 2, 1, 3).reshape(64, 2, 2304)
    field = lax.all_to_all(schur, COL, split_axis=0, concat_axis=0, tiled=True).reshape(384, 768)
    mine = lax.optimization_barrier((mine, field))[0]
    other = lax.ppermute(mine, "c", SWAP)
    core = core.reshape(1).astype(jnp.int32)
    filtered = filter_pair(core, scale_weights, weight, field, mine, other).reshape(64, 2, 2304)
    back = lax.all_to_all(filtered, ("c", "zl", "y"), split_axis=0, concat_axis=0, tiled=True)
    return final_sum(own, back.reshape(2, 4, 8, 6, 768)).transpose(1, 0, 2)


def solution(mesh):
    fine = Mesh(mesh.devices.reshape(4, 2, 4, 8, 2), MEM + COL)
    placed = (
        P(MEM, None, COL, None),
        P(None, COL, None),
        P(MEM),
        P(),
        P(None, MEM, None),
        P(None, COL, None),
    )
    return jax.shard_map(
        on_device, mesh=fine, in_specs=placed, out_specs=P(MEM, COL, None), check_vma=False
    )
```

```python
import jax
import jax.numpy as jnp
from jax import lax
from jax.experimental import pallas as pl
from jax.experimental.pallas import tpu as pltpu
from jax.sharding import Mesh, PartitionSpec as P

MEM = ("x", "zh")
COL = ("zl", "y", "c")
SWAP = [(0, 1), (1, 0)]
F32, BF16 = jnp.float32, jnp.bfloat16


VMEM = pl.BlockSpec(memory_space=pltpu.VMEM)
SMEM = pl.BlockSpec(memory_space=pltpu.SMEM)
ANY = pl.BlockSpec(memory_space=pl.ANY)
HBM = pl.BlockSpec(memory_space=pltpu.MemorySpace.HBM)


def pack_kernel(block, tiles, out):
    out[pl.ds(0, 288), :] = block[...]
    for half in range(2):
        for part in range(4):
            first = 16 * half + 4 * part
            rows = [tiles[first + n, :6, :].astype(F32) for n in range(4)]
            out[pl.ds(288 + 24 * part, 24), pl.ds(384 * half, 384)] = jnp.concatenate(rows, axis=0).astype(BF16)


def pack(block, tiles):
    return pl.pallas_call(
        pack_kernel,
        out_shape=jax.ShapeDtypeStruct((384, 768), BF16),
        in_specs=[VMEM, VMEM],
        out_specs=VMEM,
        cost_estimate=pl.CostEstimate(flops=10**6, bytes_accessed=2 * 10**6, transcendentals=0),
    )(block, tiles)


def filter_kernel(core, scale, member, field, mine, other, out, lon, lat, mid, lon_sems, lat_sems):
    lon_copies, lat_copies = [], []
    sides = ((mine, core[0]), (other, 1 - core[0]))
    for m, (part, half) in enumerate(sides):
        for s in range(3):
            for h in range(2):
                to = pl.ds(pl.multiple_of(half * 192 + 96 * h, 32), 96)
                copy = pltpu.make_async_copy(
                    part.at[s, pl.ds(288, 96), pl.ds(384 * h, 384)], lat.at[s, to, :], lat_sems.at[m, s, h]
                )
                copy.start()
                lat_copies.append(copy)
    for s in range(3):
        for m, (part, half) in enumerate(sides):
            for x in range(4):
                to = pl.ds(pl.multiple_of((2 * x + half) * 96, 32), 96)
                copy = pltpu.make_async_copy(
                    part.at[x, pl.ds(96 * s, 96), :], lon.at[s, to, :], lon_sems.at[m, s, x]
                )
                copy.start()
                lon_copies.append(copy)
    for copy in lat_copies:
        copy.wait()
    for s in range(3):
        across = jnp.dot(lat[s], field[...], preferred_element_type=F32)
        mid[s] = (scale[s] * member[0] * across).astype(BF16)
    for copy in lon_copies:
        copy.wait()
    total = jnp.zeros(out.shape, F32)
    for s in range(3):
        total += lax.dot_general(
            mid[s], lon[s], (((1,), (1,)), ((), ())), preferred_element_type=F32
        )
    out[...] = total.astype(BF16)


def filter_pair(core, scale, member, field, mine, other):
    return pl.pallas_call(
        filter_kernel,
        out_shape=jax.ShapeDtypeStruct((384, 768), BF16),
        in_specs=[SMEM, SMEM, SMEM, VMEM, HBM, HBM],
        out_specs=VMEM,
        scratch_shapes=[
            pltpu.VMEM((3, 768, 768), BF16),
            pltpu.VMEM((3, 384, 384), BF16),
            pltpu.VMEM((3, 384, 768), BF16),
            pltpu.SemaphoreType.DMA((2, 3, 4)),
            pltpu.SemaphoreType.DMA((2, 3, 2)),
        ],
        compiler_params=pltpu.CompilerParams(vmem_limit_bytes=40 * 2**20),
        cost_estimate=pl.CostEstimate(flops=2 * 10**9, bytes_accessed=5 * 10**6, transcendentals=0),
    )(core, scale, member, field, mine, other)


def final_kernel(side, own, back, keep, send):
    for out, h in ((keep, side[0]), (send, 1 - side[0])):
        for r in range(6):
            total = jnp.zeros((8, 768), F32)
            for x in range(4):
                parts = [
                    back[l % 2, x, 4 * h + l // 2, r, :].astype(F32).reshape(1, 768) for l in range(8)
                ]
                total += own[x, r, h].astype(F32) * jnp.concatenate(parts, axis=0)
            out[r] = total.astype(out.dtype)


def final_sum(side, own, back):
    return pl.pallas_call(
        final_kernel,
        out_shape=(jax.ShapeDtypeStruct((6, 8, 768), F32), jax.ShapeDtypeStruct((6, 8, 768), BF16)),
        in_specs=[SMEM, VMEM, VMEM],
        out_specs=(VMEM, VMEM),
        cost_estimate=pl.CostEstimate(flops=10**6, bytes_accessed=2 * 10**6, transcendentals=0),
    )(side, own, back)


def on_device(perturbations, gradient, member_weights, scale_weights, lon_filter, lat_filter):
    x, side, core = lax.axis_index("x"), lax.axis_index("zh"), lax.axis_index("c")
    block = lax.ppermute(lon_filter, ("zh", "c"), [(0, 0), (1, 2), (2, 1), (3, 3)])
    rows = lax.dynamic_index_in_dim(lat_filter, jnp.minimum(x, 2), 0, False)
    tiles = jnp.broadcast_to(jnp.pad(rows, ((0, 2), (0, 0)))[None], (32, 8, 384))
    tiles = lax.all_to_all(tiles, ("zl", "y"), split_axis=0, concat_axis=0, tiled=True)
    packed = pack(block.reshape(288, 768), tiles)
    mine = lax.all_gather(packed, "x", axis=0)

    own = perturbations[0].transpose(1, 0, 2).reshape(6, 4, 2, 8, 768).transpose(1, 0, 2, 3, 4)
    own = lax.all_to_all(own, "x", split_axis=0, concat_axis=0, tiled=True)
    turn = [(4 * a + b, 4 * b + a) for a in range(4) for b in range(4)]
    weight = lax.ppermute(member_weights, ("x", "zl"), turn)
    own, weight = lax.optimization_barrier((own, weight))
    level = lax.dynamic_slice_in_dim(gradient.transpose(1, 0, 2), x * 16, 16, axis=1)
    schur = (own.astype(F32) * level.reshape(1, 6, 2, 8, 768)).astype(BF16)
    schur = schur.transpose(0, 2, 3, 1, 4).reshape(64, 2, 2304)
    field = lax.all_to_all(schur, COL, split_axis=0, concat_axis=0, tiled=True).reshape(384, 768)
    mine = lax.optimization_barrier((mine, field))[0]
    other = lax.ppermute(mine, "c", SWAP)
    core = core.reshape(1).astype(jnp.int32)
    filtered = filter_pair(core, scale_weights, weight, field, mine, other).reshape(64, 2, 2304)
    back = lax.all_to_all(filtered, ("c", "zl", "y"), split_axis=0, concat_axis=0, tiled=True)
    keep, send = final_sum(side.reshape(1).astype(jnp.int32), own, back.reshape(2, 4, 8, 6, 768))
    total = keep + lax.ppermute(send, "zh", SWAP).astype(F32)
    return total.transpose(1, 0, 2)


def solution(mesh):
    fine = Mesh(mesh.devices.reshape(4, 2, 4, 8, 2), MEM + COL)
    placed = (
        P(MEM, None, COL, None),
        P(None, COL, None),
        P(MEM),
        P(),
        P(None, MEM, None),
        P(None, COL, None),
    )
    return jax.shard_map(
        on_device, mesh=fine, in_specs=placed, out_specs=P(MEM, COL, None), check_vma=False
    )
```

```python
import jax
import jax.numpy as jnp
from jax import lax
from jax.experimental import pallas as pl
from jax.experimental.pallas import tpu as pltpu
from jax.sharding import Mesh, PartitionSpec as P

MEM = ("x", "zh")
COL = ("zl", "y", "c")
SWAP = [(0, 1), (1, 0)]
F32, BF16 = jnp.float32, jnp.bfloat16


VMEM = pl.BlockSpec(memory_space=pltpu.VMEM)
SMEM = pl.BlockSpec(memory_space=pltpu.SMEM)
ANY = pl.BlockSpec(memory_space=pl.ANY)
HBM = pl.BlockSpec(memory_space=pltpu.MemorySpace.HBM)


def rows_kernel(tiles, out):
    for part in range(16):
        rows = [tiles[4 * part + n, :6, :].astype(F32) for n in range(4)]
        out[pl.ds(24 * part, 24), :] = jnp.concatenate(rows, axis=0).astype(BF16)


def join_rows(tiles):
    return pl.pallas_call(
        rows_kernel,
        out_shape=jax.ShapeDtypeStruct((384, 384), BF16),
        in_specs=[VMEM],
        out_specs=VMEM,
        cost_estimate=pl.CostEstimate(flops=10**6, bytes_accessed=6 * 10**5, transcendentals=0),
    )(tiles)


def filter_kernel(place, scale, member, field, *rest):
    rows, mine, others = rest[:4], rest[4:8], rest[8:12]
    out, lon, lat, mid, lon_sems, lat_sems = rest[12:]
    x, core = place[0], place[1]
    lon_copies, lat_copies = [], []
    for d in range(4):
        copy = pltpu.make_async_copy(rows[d], lat.at[lax.rem(x + 4 - d, 4)], lat_sems.at[d])
        copy.start()
        lat_copies.append(copy)
    for m, (part, half) in enumerate(((mine, core), (others, 1 - core))):
        for n in range(4):
            to = pl.ds(pl.multiple_of((2 * n + half) * 96, 32), 96)
            copy = pltpu.make_async_copy(part[n], lon.at[:, to, :], lon_sems.at[m, n])
            copy.start()
            lon_copies.append(copy)
    for copy in lat_copies:
        copy.wait()
    for s in range(3):
        across = jnp.dot(lat[s], field[...], preferred_element_type=F32)
        mid[s] = (scale[s] * member[0] * across).astype(BF16)
    for copy in lon_copies:
        copy.wait()
    total = jnp.zeros(out.shape, F32)
    for s in range(3):
        total += lax.dot_general(
            mid[s], lon[s], (((1,), (1,)), ((), ())), preferred_element_type=F32
        )
    out[...] = total.astype(BF16)


def filter_pair(place, scale, member, field, rows, mine, others):
    return pl.pallas_call(
        filter_kernel,
        out_shape=jax.ShapeDtypeStruct((384, 768), BF16),
        in_specs=[SMEM, SMEM, SMEM, VMEM] + [ANY] * 12,
        out_specs=VMEM,
        scratch_shapes=[
            pltpu.VMEM((3, 768, 768), BF16),
            pltpu.VMEM((4, 384, 384), BF16),
            pltpu.VMEM((3, 384, 768), BF16),
            pltpu.SemaphoreType.DMA((2, 4)),
            pltpu.SemaphoreType.DMA((4,)),
        ],
        compiler_params=pltpu.CompilerParams(vmem_limit_bytes=40 * 2**20),
        cost_estimate=pl.CostEstimate(flops=2 * 10**9, bytes_accessed=5 * 10**6, transcendentals=0),
    )(place, scale, member, field, *rows, *mine, *others)


def final_kernel(side, own, back, keep, send):
    for out, h in ((keep, side[0]), (send, 1 - side[0])):
        for r in range(6):
            total = jnp.zeros((8, 768), F32)
            for x in range(4):
                parts = [
                    back[x, 4 * h + l // 2, l % 2, r, :].astype(F32).reshape(1, 768) for l in range(8)
                ]
                total += own[x, r, h].astype(F32) * jnp.concatenate(parts, axis=0)
            out[r] = total.astype(out.dtype)


def final_sum(side, own, back):
    return pl.pallas_call(
        final_kernel,
        out_shape=(jax.ShapeDtypeStruct((6, 8, 768), F32), jax.ShapeDtypeStruct((6, 8, 768), BF16)),
        in_specs=[SMEM, VMEM, VMEM],
        out_specs=(VMEM, VMEM),
        cost_estimate=pl.CostEstimate(flops=10**6, bytes_accessed=2 * 10**6, transcendentals=0),
    )(side, own, back)


def on_device(perturbations, gradient, member_weights, scale_weights, lon_filter, lat_filter):
    x, side, core = lax.axis_index("x"), lax.axis_index("zh"), lax.axis_index("c")
    block = lax.ppermute(lon_filter, ("zh", "c"), [(0, 0), (1, 2), (2, 1), (3, 3)])
    rows = lax.dynamic_index_in_dim(lat_filter, jnp.minimum(x, 2), 0, False)
    tiles = jnp.broadcast_to(jnp.pad(rows, ((0, 2), (0, 0)))[None], (64, 8, 384))
    rows = join_rows(lax.all_to_all(tiles, COL, split_axis=0, concat_axis=0, tiled=True))
    rows = [rows] + [
        lax.ppermute(rows, "x", [(i, (i + d) % 4) for i in range(4)]) for d in (1, 2, 3)
    ]

    own = perturbations[0].transpose(1, 0, 2).reshape(6, 4, 2, 8, 768).transpose(1, 0, 2, 3, 4)
    own = lax.all_to_all(own, "x", split_axis=0, concat_axis=0, tiled=True)
    turn = [(4 * a + b, 4 * b + a) for a in range(4) for b in range(4)]
    weight = lax.ppermute(member_weights, ("x", "zl"), turn)
    own, weight, block = lax.optimization_barrier((own, weight, block))
    mine = lax.all_gather(block, "x", axis=0)
    level = lax.dynamic_slice_in_dim(gradient.transpose(1, 0, 2), x * 16, 16, axis=1)
    schur = (own.astype(F32) * level.reshape(1, 6, 2, 8, 768)).astype(BF16)
    schur = schur.transpose(0, 2, 3, 1, 4).reshape(64, 2, 2304)
    field = lax.all_to_all(schur, COL, split_axis=0, concat_axis=0, tiled=True).reshape(384, 768)
    mine = lax.optimization_barrier((mine, schur))[0]
    mine = [mine[n] for n in range(4)]
    others = [lax.ppermute(part, "c", SWAP) for part in mine]
    place = jnp.stack([x, core]).astype(jnp.int32)
    filtered = filter_pair(place, scale_weights, weight, field, rows, mine, others)
    back = lax.all_to_all(filtered.reshape(64, 2, 2304), COL, split_axis=0, concat_axis=0, tiled=True)
    keep, send = final_sum(side.reshape(1).astype(jnp.int32), own, back.reshape(4, 8, 2, 6, 768))
    total = keep + lax.ppermute(send, "zh", SWAP).astype(F32)
    return total.transpose(1, 0, 2)


def solution(mesh):
    fine = Mesh(mesh.devices.reshape(4, 2, 4, 8, 2), MEM + COL)
    placed = (
        P(MEM, None, COL, None),
        P(None, COL, None),
        P(MEM),
        P(),
        P(None, MEM, None),
        P(None, COL, None),
    )
    return jax.shard_map(
        on_device, mesh=fine, in_specs=placed, out_specs=P(MEM, COL, None), check_vma=False
    )
```

```python
import jax
import jax.numpy as jnp
from jax import lax
from jax.experimental import pallas as pl
from jax.experimental.pallas import tpu as pltpu
from jax.sharding import Mesh, PartitionSpec as P

MEM = ("x", "zh")
COL = ("zl", "y", "c")
SWAP = [(0, 1), (1, 0)]
F32, BF16 = jnp.float32, jnp.bfloat16


VMEM = pl.BlockSpec(memory_space=pltpu.VMEM)
SMEM = pl.BlockSpec(memory_space=pltpu.SMEM)
ANY = pl.BlockSpec(memory_space=pl.ANY)
HBM = pl.BlockSpec(memory_space=pltpu.MemorySpace.HBM)


def pack_kernel(block, tiles, out):
    out[pl.ds(0, 288), :] = block[...]
    for half in range(2):
        for part in range(4):
            first = 16 * half + 4 * part
            rows = [tiles[first + n, :6, :].astype(F32) for n in range(4)]
            out[pl.ds(288 + 24 * part, 24), pl.ds(384 * half, 384)] = jnp.concatenate(rows, axis=0).astype(BF16)


def pack(block, tiles):
    return pl.pallas_call(
        pack_kernel,
        out_shape=jax.ShapeDtypeStruct((384, 768), BF16),
        in_specs=[VMEM, VMEM],
        out_specs=VMEM,
        compiler_params=pltpu.CompilerParams(vmem_limit_bytes=16 * 2**20),
        cost_estimate=pl.CostEstimate(flops=10**6, bytes_accessed=2 * 10**6, transcendentals=0),
    )(block, tiles)


def filter_kernel(core, scale, member, field, mine, other, out, lon, lat, mid, lon_sems, lat_sems):
    lon_copies, lat_copies = [], []
    sides = ((mine, core[0]), (other, 1 - core[0]))
    for m, (part, half) in enumerate(sides):
        for s in range(3):
            for h in range(2):
                to = pl.ds(pl.multiple_of(half * 192 + 96 * h, 32), 96)
                copy = pltpu.make_async_copy(
                    part.at[s, pl.ds(288, 96), pl.ds(384 * h, 384)], lat.at[s, to, :], lat_sems.at[m, s, h]
                )
                copy.start()
                lat_copies.append(copy)
    for s in range(3):
        for m, (part, half) in enumerate(sides):
            for x in range(4):
                to = pl.ds(pl.multiple_of((2 * x + half) * 96, 32), 96)
                copy = pltpu.make_async_copy(
                    part.at[x, pl.ds(96 * s, 96), :], lon.at[to, pl.ds(768 * s, 768)], lon_sems.at[m, s, x]
                )
                copy.start()
                lon_copies.append(copy)
    for copy in lat_copies:
        copy.wait()
    for s in range(3):
        across = jnp.dot(lat[s], field[...], preferred_element_type=F32)
        mid[:, pl.ds(768 * s, 768)] = (scale[s] * member[0] * across).astype(BF16)
    for copy in lon_copies:
        copy.wait()
    total = lax.dot_general(
        mid[...], lon[...], (((1,), (1,)), ((), ())), preferred_element_type=F32
    )
    out[...] = total.astype(BF16)


def filter_pair(core, scale, member, field, mine, other):
    return pl.pallas_call(
        filter_kernel,
        out_shape=jax.ShapeDtypeStruct((384, 768), BF16),
        in_specs=[SMEM, SMEM, SMEM, VMEM, HBM, HBM],
        out_specs=VMEM,
        scratch_shapes=[
            pltpu.VMEM((768, 2304), BF16),
            pltpu.VMEM((3, 384, 384), BF16),
            pltpu.VMEM((384, 2304), BF16),
            pltpu.SemaphoreType.DMA((2, 3, 4)),
            pltpu.SemaphoreType.DMA((2, 3, 2)),
        ],
        compiler_params=pltpu.CompilerParams(vmem_limit_bytes=40 * 2**20),
        cost_estimate=pl.CostEstimate(flops=2 * 10**9, bytes_accessed=5 * 10**6, transcendentals=0),
    )(core, scale, member, field, mine, other)


def member_sum(own, back, h, r):
    total = jnp.zeros((8, 768), F32)
    for x in range(4):
        parts = [back[l % 2, x, 4 * h + l // 2, r, :].astype(F32).reshape(1, 768) for l in range(8)]
        total += own[x, r, h].astype(F32) * jnp.concatenate(parts, axis=0)
    return total


def send_kernel(side, own, back, out):
    for r in range(6):
        out[r] = member_sum(own, back, 1 - side[0], r).astype(out.dtype)


def keep_kernel(side, own, back, other, out):
    for r in range(6):
        out[r] = member_sum(own, back, side[0], r) + other[r].astype(F32)


def final_sum(side, own, back):
    common = dict(
        compiler_params=pltpu.CompilerParams(vmem_limit_bytes=16 * 2**20),
        cost_estimate=pl.CostEstimate(flops=10**6, bytes_accessed=10**6, transcendentals=0),
    )
    send = pl.pallas_call(
        send_kernel,
        out_shape=jax.ShapeDtypeStruct((6, 8, 768), BF16),
        in_specs=[SMEM, VMEM, VMEM],
        out_specs=VMEM,
        **common,
    )(side, own, back)
    return pl.pallas_call(
        keep_kernel,
        out_shape=jax.ShapeDtypeStruct((6, 8, 768), F32),
        in_specs=[SMEM, VMEM, VMEM, VMEM],
        out_specs=VMEM,
        **common,
    )(side, own, back, lax.ppermute(send, "zh", SWAP))


def on_device(perturbations, gradient, member_weights, scale_weights, lon_filter, lat_filter):
    x, side, core = lax.axis_index("x"), lax.axis_index("zh"), lax.axis_index("c")
    pairs = [(8 * h + 2 * z + h, 8 * h + 2 * z + h) for h in range(2) for z in range(4)]
    pairs += [(8 * h + 2 * z + 1 - h, 8 * (1 - h) + 2 * (3 - z) + h) for h in range(2) for z in range(4)]
    block = lax.ppermute(lon_filter, ("zh", "zl", "c"), pairs)
    rows = lax.dynamic_index_in_dim(lat_filter, jnp.minimum(x, 2), 0, False)
    tiles = jnp.broadcast_to(jnp.pad(rows, ((0, 2), (0, 0)))[None], (32, 8, 384))
    tiles = lax.all_to_all(tiles, ("zl", "y"), split_axis=0, concat_axis=0, tiled=True)
    packed = pack(block.reshape(288, 768), tiles)
    mine = lax.all_gather(packed, "x", axis=0)

    own = perturbations[0].transpose(1, 0, 2).reshape(6, 4, 2, 8, 768).transpose(1, 0, 2, 3, 4)
    own = lax.all_to_all(own, "x", split_axis=0, concat_axis=0, tiled=True)
    turn = [(4 * a + b, 4 * b + a) for a in range(4) for b in range(4)]
    weight = lax.ppermute(member_weights, ("x", "zl"), turn)
    own, weight = lax.optimization_barrier((own, weight))
    level = lax.dynamic_slice_in_dim(gradient.transpose(1, 0, 2), x * 16, 16, axis=1)
    schur = (own.astype(F32) * level.reshape(1, 6, 2, 8, 768)).astype(BF16)
    schur = schur.transpose(0, 2, 3, 1, 4).reshape(64, 2, 2304)
    field = lax.all_to_all(schur, COL, split_axis=0, concat_axis=0, tiled=True).reshape(384, 768)
    mine = lax.optimization_barrier((mine, field))[0]
    other = lax.ppermute(mine, "c", SWAP)
    core = core.reshape(1).astype(jnp.int32)
    filtered = filter_pair(core, scale_weights, weight, field, mine, other).reshape(64, 2, 2304)
    back = lax.all_to_all(filtered, ("c", "zl", "y"), split_axis=0, concat_axis=0, tiled=True)
    total = final_sum(side.reshape(1).astype(jnp.int32), own, back.reshape(2, 4, 8, 6, 768))
    return total.transpose(1, 0, 2)


def solution(mesh):
    fine = Mesh(mesh.devices.reshape(4, 2, 4, 8, 2), MEM + COL)
    placed = (
        P(MEM, None, COL, None),
        P(None, COL, None),
        P(MEM),
        P(),
        P(None, MEM, None),
        P(None, COL, None),
    )
    return jax.shard_map(
        on_device, mesh=fine, in_specs=placed, out_specs=P(MEM, COL, None), check_vma=False
    )
```

```python
import jax
import jax.numpy as jnp
from jax import lax
from jax.experimental import pallas as pl
from jax.experimental.pallas import tpu as pltpu
from jax.sharding import Mesh, PartitionSpec as P

MEM = ("x", "zh")
COL = ("zl", "y", "c")
SWAP = [(0, 1), (1, 0)]
F32, BF16 = jnp.float32, jnp.bfloat16


VMEM = pl.BlockSpec(memory_space=pltpu.VMEM)
SMEM = pl.BlockSpec(memory_space=pltpu.SMEM)
ANY = pl.BlockSpec(memory_space=pl.ANY)
HBM = pl.BlockSpec(memory_space=pltpu.MemorySpace.HBM)


def pack_kernel(one, two, three, tiles, out):
    for s, block in enumerate((one, two, three)):
        out[pl.ds(96 * s, 96), :] = block[...]
    for half in range(2):
        for part in range(4):
            first = 16 * half + 4 * part
            rows = [tiles[first + n, :6, :].astype(F32) for n in range(4)]
            out[pl.ds(288 + 24 * part, 24), pl.ds(384 * half, 384)] = jnp.concatenate(rows, axis=0).astype(BF16)


def pack(blocks, tiles):
    return pl.pallas_call(
        pack_kernel,
        out_shape=jax.ShapeDtypeStruct((384, 768), BF16),
        in_specs=[VMEM] * 4,
        out_specs=VMEM,
        compiler_params=pltpu.CompilerParams(vmem_limit_bytes=16 * 2**20),
        cost_estimate=pl.CostEstimate(flops=10**6, bytes_accessed=2 * 10**6, transcendentals=0),
    )(*blocks, tiles)


def filter_kernel(core, scale, member, field, mine, other, out, lon, lat, mid, lon_sems, lat_sems):
    lon_copies, lat_copies = [], []
    sides = ((mine, core[0]), (other, 1 - core[0]))
    for m, (part, half) in enumerate(sides):
        for s in range(3):
            for h in range(2):
                to = pl.ds(pl.multiple_of(half * 192 + 96 * h, 32), 96)
                copy = pltpu.make_async_copy(
                    part.at[s, pl.ds(288, 96), pl.ds(384 * h, 384)], lat.at[s, to, :], lat_sems.at[m, s, h]
                )
                copy.start()
                lat_copies.append(copy)
    for s in range(3):
        for m, (part, half) in enumerate(sides):
            for x in range(4):
                to = pl.ds(pl.multiple_of((2 * x + half) * 96, 32), 96)
                copy = pltpu.make_async_copy(
                    part.at[x, pl.ds(96 * s, 96), :], lon.at[to, pl.ds(768 * s, 768)], lon_sems.at[m, s, x]
                )
                copy.start()
                lon_copies.append(copy)
    for copy in lat_copies:
        copy.wait()
    for s in range(3):
        across = jnp.dot(lat[s], field[...], preferred_element_type=F32)
        mid[:, pl.ds(768 * s, 768)] = (scale[s] * member[0] * across).astype(BF16)
    for copy in lon_copies:
        copy.wait()
    total = lax.dot_general(
        mid[...], lon[...], (((1,), (1,)), ((), ())), preferred_element_type=F32
    )
    out[...] = total.astype(BF16)


def filter_pair(core, scale, member, field, mine, other):
    return pl.pallas_call(
        filter_kernel,
        out_shape=jax.ShapeDtypeStruct((384, 768), BF16),
        in_specs=[SMEM, SMEM, SMEM, VMEM, HBM, HBM],
        out_specs=VMEM,
        scratch_shapes=[
            pltpu.VMEM((768, 2304), BF16),
            pltpu.VMEM((3, 384, 384), BF16),
            pltpu.VMEM((384, 2304), BF16),
            pltpu.SemaphoreType.DMA((2, 3, 4)),
            pltpu.SemaphoreType.DMA((2, 3, 2)),
        ],
        compiler_params=pltpu.CompilerParams(vmem_limit_bytes=40 * 2**20),
        cost_estimate=pl.CostEstimate(flops=2 * 10**9, bytes_accessed=5 * 10**6, transcendentals=0),
    )(core, scale, member, field, mine, other)


def member_sum(own, back, h, r):
    total = jnp.zeros((8, 768), F32)
    for x in range(4):
        parts = [back[l % 2, x, 4 * h + l // 2, r, :].astype(F32).reshape(1, 768) for l in range(8)]
        total += own[x, r, h].astype(F32) * jnp.concatenate(parts, axis=0)
    return total


def send_kernel(side, own, back, out):
    for r in range(6):
        out[r] = member_sum(own, back, 1 - side[0], r).astype(out.dtype)


def keep_kernel(side, own, back, other, out):
    for r in range(6):
        out[r] = member_sum(own, back, side[0], r) + other[r].astype(F32)


def final_sum(side, own, back):
    common = dict(
        compiler_params=pltpu.CompilerParams(vmem_limit_bytes=16 * 2**20),
        cost_estimate=pl.CostEstimate(flops=10**6, bytes_accessed=10**6, transcendentals=0),
    )
    send = pl.pallas_call(
        send_kernel,
        out_shape=jax.ShapeDtypeStruct((6, 8, 768), BF16),
        in_specs=[SMEM, VMEM, VMEM],
        out_specs=VMEM,
        **common,
    )(side, own, back)
    return pl.pallas_call(
        keep_kernel,
        out_shape=jax.ShapeDtypeStruct((6, 8, 768), F32),
        in_specs=[SMEM, VMEM, VMEM, VMEM],
        out_specs=VMEM,
        **common,
    )(side, own, back, lax.ppermute(send, "zh", SWAP))


def on_device(perturbations, gradient, member_weights, scale_weights, lon_filter, lat_filter):
    x, side, core = lax.axis_index("x"), lax.axis_index("zh"), lax.axis_index("c")
    rows = lax.dynamic_index_in_dim(lat_filter, jnp.minimum(x, 2), 0, False)
    tiles = jnp.broadcast_to(jnp.pad(rows, ((0, 2), (0, 0)))[None], (32, 8, 384))
    tiles, lon_filter = lax.optimization_barrier((tiles, lon_filter))
    pairs = [(8 * h + 2 * z + h, 8 * h + 2 * z + h) for h in range(2) for z in range(4)]
    pairs += [(8 * h + 2 * z + 1 - h, 8 * (1 - h) + 2 * (3 - z) + h) for h in range(2) for z in range(4)]
    blocks = [lax.ppermute(lon_filter[s], ("zh", "zl", "c"), pairs) for s in range(3)]
    tiles = lax.all_to_all(tiles, ("zl", "y"), split_axis=0, concat_axis=0, tiled=True)
    packed = pack(blocks, tiles)
    mine = lax.all_gather(packed, "x", axis=0)

    own = perturbations[0].transpose(1, 0, 2).reshape(6, 4, 2, 8, 768).transpose(1, 0, 2, 3, 4)
    own = lax.all_to_all(own, "x", split_axis=0, concat_axis=0, tiled=True)
    turn = [(4 * a + b, 4 * b + a) for a in range(4) for b in range(4)]
    weight = lax.ppermute(member_weights, ("x", "zl"), turn)
    core, side = core.reshape(1).astype(jnp.int32), side.reshape(1).astype(jnp.int32)
    own, weight, core, side = lax.optimization_barrier((own, weight, core, side))
    level = lax.dynamic_slice_in_dim(gradient.transpose(1, 0, 2), x * 16, 16, axis=1)
    schur = (own.astype(F32) * level.reshape(1, 6, 2, 8, 768)).astype(BF16)
    schur = schur.transpose(0, 2, 3, 1, 4).reshape(64, 2, 2304)
    field = lax.all_to_all(schur, COL, split_axis=0, concat_axis=0, tiled=True).reshape(384, 768)
    mine = lax.optimization_barrier((mine, field))[0]
    other = lax.ppermute(mine, "c", SWAP)
    filtered = filter_pair(core, scale_weights, weight, field, mine, other).reshape(64, 2, 2304)
    back = lax.all_to_all(filtered, ("c", "zl", "y"), split_axis=0, concat_axis=0, tiled=True)
    total = final_sum(side, own, back.reshape(2, 4, 8, 6, 768))
    return total.transpose(1, 0, 2)


def solution(mesh):
    fine = Mesh(mesh.devices.reshape(4, 2, 4, 8, 2), MEM + COL)
    placed = (
        P(MEM, None, COL, None),
        P(None, COL, None),
        P(MEM),
        P(),
        P(None, MEM, None),
        P(None, COL, None),
    )
    return jax.shard_map(
        on_device, mesh=fine, in_specs=placed, out_specs=P(MEM, COL, None), check_vma=False
    )
```

```python
import jax
import jax.numpy as jnp
from jax import lax
from jax.experimental import pallas as pl
from jax.experimental.pallas import tpu as pltpu
from jax.sharding import Mesh, PartitionSpec as P

MEM = ("x", "zh")
COL = ("zl", "y", "c")
SWAP = [(0, 1), (1, 0)]
F32, BF16 = jnp.float32, jnp.bfloat16


VMEM = pl.BlockSpec(memory_space=pltpu.VMEM)
SMEM = pl.BlockSpec(memory_space=pltpu.SMEM)
ANY = pl.BlockSpec(memory_space=pl.ANY)
HBM = pl.BlockSpec(memory_space=pltpu.MemorySpace.HBM)


def pack_kernel(block, tiles, out):
    out[pl.ds(0, 288), :] = block[...]
    for half in range(2):
        for part in range(4):
            first = 16 * half + 4 * part
            rows = [tiles[first + n, :6, :].astype(F32) for n in range(4)]
            out[pl.ds(288 + 24 * part, 24), pl.ds(384 * half, 384)] = jnp.concatenate(rows, axis=0).astype(BF16)


def pack(block, tiles):
    return pl.pallas_call(
        pack_kernel,
        out_shape=jax.ShapeDtypeStruct((384, 768), BF16),
        in_specs=[VMEM, VMEM],
        out_specs=VMEM,
        compiler_params=pltpu.CompilerParams(vmem_limit_bytes=16 * 2**20),
        cost_estimate=pl.CostEstimate(flops=10**6, bytes_accessed=2 * 10**6, transcendentals=0),
    )(block, tiles)


def filter_kernel(core, scale, member, field, mine, other, out, lon, lat, mid, lon_sems, lat_sems):
    lon_copies, lat_copies = [], []
    sides = ((mine, core[0]), (other, 1 - core[0]))
    for m, (part, half) in enumerate(sides):
        for s in range(3):
            for h in range(2):
                to = pl.ds(pl.multiple_of(half * 192 + 96 * h, 32), 96)
                copy = pltpu.make_async_copy(
                    part.at[s, pl.ds(288, 96), pl.ds(384 * h, 384)], lat.at[s, to, :], lat_sems.at[m, s, h]
                )
                copy.start()
                lat_copies.append(copy)
    for s in range(3):
        for m, (part, half) in enumerate(sides):
            for x in range(4):
                to = pl.ds(pl.multiple_of((2 * x + half) * 96, 32), 96)
                copy = pltpu.make_async_copy(
                    part.at[x, pl.ds(96 * s, 96), :], lon.at[to, pl.ds(768 * s, 768)], lon_sems.at[m, s, x]
                )
                copy.start()
                lon_copies.append(copy)
    for copy in lat_copies:
        copy.wait()
    for s in range(3):
        across = jnp.dot(lat[s], field[...], preferred_element_type=F32)
        mid[:, pl.ds(768 * s, 768)] = (scale[s] * member[0] * across).astype(BF16)
    for copy in lon_copies:
        copy.wait()
    total = lax.dot_general(
        mid[...], lon[...], (((1,), (1,)), ((), ())), preferred_element_type=F32
    )
    out[...] = total.astype(BF16)


def filter_pair(core, scale, member, field, mine, other):
    return pl.pallas_call(
        filter_kernel,
        out_shape=jax.ShapeDtypeStruct((384, 768), BF16),
        in_specs=[SMEM, SMEM, SMEM, VMEM, HBM, HBM],
        out_specs=VMEM,
        scratch_shapes=[
            pltpu.VMEM((768, 2304), BF16),
            pltpu.VMEM((3, 384, 384), BF16),
            pltpu.VMEM((384, 2304), BF16),
            pltpu.SemaphoreType.DMA((2, 3, 4)),
            pltpu.SemaphoreType.DMA((2, 3, 2)),
        ],
        compiler_params=pltpu.CompilerParams(vmem_limit_bytes=40 * 2**20),
        cost_estimate=pl.CostEstimate(flops=2 * 10**9, bytes_accessed=5 * 10**6, transcendentals=0),
    )(core, scale, member, field, mine, other)


def member_sum(own, back, h, r):
    total = jnp.zeros((8, 768), F32)
    for x in range(4):
        parts = [back[l % 2, x, 4 * h + l // 2, r, :].astype(F32).reshape(1, 768) for l in range(8)]
        total += own[x, r, h].astype(F32) * jnp.concatenate(parts, axis=0)
    return total


def send_kernel(side, own, back, out):
    for r in range(6):
        out[r] = member_sum(own, back, 1 - side[0], r).astype(out.dtype)


def keep_kernel(side, own, back, other, out):
    for r in range(6):
        out[r] = member_sum(own, back, side[0], r) + other[r].astype(F32)


def final_sum(side, own, back):
    common = dict(
        compiler_params=pltpu.CompilerParams(vmem_limit_bytes=16 * 2**20),
        cost_estimate=pl.CostEstimate(flops=10**6, bytes_accessed=10**6, transcendentals=0),
    )
    send = pl.pallas_call(
        send_kernel,
        out_shape=jax.ShapeDtypeStruct((6, 8, 768), BF16),
        in_specs=[SMEM, VMEM, VMEM],
        out_specs=VMEM,
        **common,
    )(side, own, back)
    return pl.pallas_call(
        keep_kernel,
        out_shape=jax.ShapeDtypeStruct((6, 8, 768), F32),
        in_specs=[SMEM, VMEM, VMEM, VMEM],
        out_specs=VMEM,
        **common,
    )(side, own, back, lax.ppermute(send, "zh", SWAP))


def on_device(perturbations, gradient, member_weights, scale_weights, lon_filter, lat_filter):
    x, side, core = lax.axis_index("x"), lax.axis_index("zh"), lax.axis_index("c")
    pairs = [(8 * h + 2 * z + h, 8 * h + 2 * z + h) for h in range(2) for z in range(4)]
    pairs += [(8 * h + 2 * z + 1 - h, 8 * (1 - h) + 2 * (3 - z) + h) for h in range(2) for z in range(4)]
    block = lax.ppermute(lon_filter, ("zh", "zl", "c"), pairs)
    rows = lax.dynamic_index_in_dim(lat_filter, jnp.minimum(x, 2), 0, False)
    tiles = jnp.broadcast_to(jnp.pad(rows, ((0, 2), (0, 0)))[None], (32, 8, 384))
    tiles = lax.all_to_all(tiles, ("zl", "y"), split_axis=0, concat_axis=0, tiled=True)
    packed = pack(block.reshape(288, 768), tiles)
    mine = lax.all_gather(packed, "x", axis=0)

    own = perturbations[0].transpose(1, 0, 2).reshape(6, 4, 2, 8, 768).transpose(1, 0, 2, 3, 4)
    own = lax.all_to_all(own, "x", split_axis=0, concat_axis=0, tiled=True)
    core, side = core.reshape(1).astype(jnp.int32), side.reshape(1).astype(jnp.int32)
    own, core, side = lax.optimization_barrier((own, core, side))
    turn = [(4 * a + b, 4 * b + a) for a in range(4) for b in range(4)]
    weight = lax.optimization_barrier((member_weights, own))[0]
    weight = lax.ppermute(weight, ("x", "zl"), turn)
    level = lax.dynamic_slice_in_dim(gradient.transpose(1, 0, 2), x * 16, 16, axis=1)
    schur = (own.astype(F32) * level.reshape(1, 6, 2, 8, 768)).astype(BF16)
    schur = schur.transpose(0, 2, 3, 1, 4).reshape(64, 2, 2304)
    field = lax.all_to_all(schur, COL, split_axis=0, concat_axis=0, tiled=True).reshape(384, 768)
    mine = lax.optimization_barrier((mine, field))[0]
    other = lax.ppermute(mine, "c", SWAP)
    filtered = filter_pair(core, scale_weights, weight, field, mine, other).reshape(64, 2, 2304)
    back = lax.all_to_all(filtered, ("c", "zl", "y"), split_axis=0, concat_axis=0, tiled=True)
    total = final_sum(side, own, back.reshape(2, 4, 8, 6, 768))
    return total.transpose(1, 0, 2)


def solution(mesh):
    fine = Mesh(mesh.devices.reshape(4, 2, 4, 8, 2), MEM + COL)
    placed = (
        P(MEM, None, COL, None),
        P(None, COL, None),
        P(MEM),
        P(),
        P(None, MEM, None),
        P(None, COL, None),
    )
    return jax.shard_map(
        on_device, mesh=fine, in_specs=placed, out_specs=P(MEM, COL, None), check_vma=False
    )
```

```python
import jax
import jax.numpy as jnp
from jax import lax
from jax.experimental import pallas as pl
from jax.experimental.pallas import tpu as pltpu
from jax.sharding import Mesh, PartitionSpec as P

MEM = ("x", "zh")
COL = ("zl", "y", "c")
SWAP = [(0, 1), (1, 0)]
F32, BF16 = jnp.float32, jnp.bfloat16


VMEM = pl.BlockSpec(memory_space=pltpu.VMEM)
SMEM = pl.BlockSpec(memory_space=pltpu.SMEM)
ANY = pl.BlockSpec(memory_space=pl.ANY)
HBM = pl.BlockSpec(memory_space=pltpu.MemorySpace.HBM)


def pack_kernel(block, tiles, out):
    out[pl.ds(0, 288), :] = block[...]
    for half in range(2):
        for part in range(4):
            first = 16 * half + 4 * part
            rows = [tiles[first + n, :6, :].astype(F32) for n in range(4)]
            out[pl.ds(288 + 24 * part, 24), pl.ds(384 * half, 384)] = jnp.concatenate(rows, axis=0).astype(BF16)


def pack(block, tiles):
    return pl.pallas_call(
        pack_kernel,
        out_shape=jax.ShapeDtypeStruct((384, 768), BF16),
        in_specs=[VMEM, VMEM],
        out_specs=VMEM,
        compiler_params=pltpu.CompilerParams(vmem_limit_bytes=16 * 2**20),
        cost_estimate=pl.CostEstimate(flops=10**6, bytes_accessed=2 * 10**6, transcendentals=0),
    )(block, tiles)


def filter_kernel(core, scale, member, field, mine, other, out, lon, lat, mid, lon_sems, lat_sems):
    lon_copies, lat_copies = [], []
    sides = ((mine, core[0]), (other, 1 - core[0]))
    for m, (part, half) in enumerate(sides):
        for s in range(3):
            for h in range(2):
                to = pl.ds(pl.multiple_of(half * 192 + 96 * h, 32), 96)
                copy = pltpu.make_async_copy(
                    part.at[s, pl.ds(288, 96), pl.ds(384 * h, 384)], lat.at[s, to, :], lat_sems.at[m, s, h]
                )
                copy.start()
                lat_copies.append(copy)
    for s in range(3):
        for m, (part, half) in enumerate(sides):
            for x in range(4):
                to = pl.ds(pl.multiple_of((2 * x + half) * 96, 32), 96)
                copy = pltpu.make_async_copy(
                    part.at[x, pl.ds(96 * s, 96), :], lon.at[to, pl.ds(768 * s, 768)], lon_sems.at[m, s, x]
                )
                copy.start()
                lon_copies.append(copy)
    for copy in lat_copies:
        copy.wait()
    for s in range(3):
        across = jnp.dot(lat[s], field[...], preferred_element_type=F32)
        mid[:, pl.ds(768 * s, 768)] = (scale[s] * member[0] * across).astype(BF16)
    for copy in lon_copies:
        copy.wait()
    total = lax.dot_general(
        mid[...], lon[...], (((1,), (1,)), ((), ())), preferred_element_type=F32
    )
    out[...] = total.astype(BF16)


def filter_pair(core, scale, member, field, mine, other):
    return pl.pallas_call(
        filter_kernel,
        out_shape=jax.ShapeDtypeStruct((384, 768), BF16),
        in_specs=[SMEM, SMEM, SMEM, VMEM, HBM, HBM],
        out_specs=VMEM,
        scratch_shapes=[
            pltpu.VMEM((768, 2304), BF16),
            pltpu.VMEM((3, 384, 384), BF16),
            pltpu.VMEM((384, 2304), BF16),
            pltpu.SemaphoreType.DMA((2, 3, 4)),
            pltpu.SemaphoreType.DMA((2, 3, 2)),
        ],
        compiler_params=pltpu.CompilerParams(vmem_limit_bytes=40 * 2**20),
        cost_estimate=pl.CostEstimate(flops=2 * 10**9, bytes_accessed=5 * 10**6, transcendentals=0),
    )(core, scale, member, field, mine, other)


def member_sum(own, back, h, r):
    total = jnp.zeros((8, 768), F32)
    for x in range(4):
        parts = [back[l % 2, x, 4 * h + l // 2, r, :].astype(F32).reshape(1, 768) for l in range(8)]
        total += own[x, r, h].astype(F32) * jnp.concatenate(parts, axis=0)
    return total


def send_kernel(side, own, back, out):
    for r in range(6):
        out[r] = member_sum(own, back, 1 - side[0], r).astype(out.dtype)


def keep_kernel(side, own, back, other, out):
    for r in range(6):
        out[r] = member_sum(own, back, side[0], r) + other[r].astype(F32)


def final_sum(side, own, back):
    common = dict(
        compiler_params=pltpu.CompilerParams(vmem_limit_bytes=16 * 2**20),
        cost_estimate=pl.CostEstimate(flops=10**6, bytes_accessed=10**6, transcendentals=0),
    )
    send = pl.pallas_call(
        send_kernel,
        out_shape=jax.ShapeDtypeStruct((6, 8, 768), BF16),
        in_specs=[SMEM, VMEM, VMEM],
        out_specs=VMEM,
        **common,
    )(side, own, back)
    return pl.pallas_call(
        keep_kernel,
        out_shape=jax.ShapeDtypeStruct((6, 8, 768), F32),
        in_specs=[SMEM, VMEM, VMEM, VMEM],
        out_specs=VMEM,
        **common,
    )(side, own, back, lax.ppermute(send, "zh", SWAP))


def on_device(perturbations, gradient, member_weights, scale_weights, lon_filter, lat_filter):
    x, side, core = lax.axis_index("x"), lax.axis_index("zh"), lax.axis_index("c")
    pairs = [(8 * h + 2 * z + h, 8 * h + 2 * z + h) for h in range(2) for z in range(4)]
    pairs += [(8 * h + 2 * z + 1 - h, 8 * (1 - h) + 2 * (3 - z) + h) for h in range(2) for z in range(4)]
    block = lax.ppermute(lon_filter, ("zh", "zl", "c"), pairs)
    rows = lax.dynamic_index_in_dim(lat_filter, jnp.minimum(x, 2), 0, False)
    tiles = jnp.broadcast_to(jnp.pad(rows, ((0, 2), (0, 0)))[None], (32, 8, 384))
    tiles = lax.all_to_all(tiles, ("zl", "y"), split_axis=0, concat_axis=0, tiled=True)
    packed = pack(block.reshape(288, 768), tiles)
    mine = lax.all_gather(packed, "x", axis=0)

    own = perturbations[0].transpose(1, 0, 2).reshape(6, 4, 2, 8, 768).transpose(1, 0, 2, 3, 4)
    own = lax.all_to_all(own, "x", split_axis=0, concat_axis=0, tiled=True)
    turn = [(4 * a + b, 4 * b + a) for a in range(4) for b in range(4)]
    weight = lax.ppermute(member_weights, ("x", "zl"), turn)
    core, side = core.reshape(1).astype(jnp.int32), side.reshape(1).astype(jnp.int32)
    own, weight, core, side = lax.optimization_barrier((own, weight, core, side))
    level = lax.dynamic_slice_in_dim(gradient.transpose(1, 0, 2), x * 16, 16, axis=1)
    schur = (own.astype(F32) * level.reshape(1, 6, 2, 8, 768)).astype(BF16)
    schur = schur.transpose(0, 2, 3, 1, 4).reshape(64, 2, 2304)
    field = lax.all_to_all(schur, COL, split_axis=0, concat_axis=0, tiled=True).reshape(384, 768)
    mine = lax.optimization_barrier((mine, field))[0]
    other = lax.ppermute(mine, "c", SWAP)
    filtered = filter_pair(core, scale_weights, weight, field, mine, other).reshape(64, 2, 2304)
    back = lax.all_to_all(filtered, ("c", "zl", "y"), split_axis=0, concat_axis=0, tiled=True)
    total = final_sum(side, own, back.reshape(2, 4, 8, 6, 768))
    return total.transpose(1, 0, 2)


def solution(mesh):
    fine = Mesh(mesh.devices.reshape(4, 2, 4, 8, 2), MEM + COL)
    placed = (
        P(MEM, None, COL, None),
        P(None, COL, None),
        P(MEM),
        P(),
        P(None, MEM, None),
        P(None, COL, None),
    )
    return jax.shard_map(
        on_device, mesh=fine, in_specs=placed, out_specs=P(MEM, COL, None), check_vma=False
    )
```

```python
import jax
import jax.numpy as jnp
from jax import lax
from jax.experimental import pallas as pl
from jax.experimental.pallas import tpu as pltpu
from jax.sharding import Mesh, PartitionSpec as P

MEM = ("x", "zh")
COL = ("zl", "y", "c")
SWAP = [(0, 1), (1, 0)]
F32, BF16 = jnp.float32, jnp.bfloat16


VMEM = pl.BlockSpec(memory_space=pltpu.VMEM)
SMEM = pl.BlockSpec(memory_space=pltpu.SMEM)
ANY = pl.BlockSpec(memory_space=pl.ANY)


def pack_kernel(block, tiles, out):
    out[pl.ds(0, 288), :] = block[...]
    for half in range(2):
        for part in range(4):
            first = 16 * half + 4 * part
            rows = [tiles[first + n, :6, :].astype(F32) for n in range(4)]
            out[pl.ds(288 + 24 * part, 24), pl.ds(384 * half, 384)] = jnp.concatenate(rows, axis=0).astype(BF16)


def pack(block, tiles):
    return pl.pallas_call(
        pack_kernel,
        out_shape=jax.ShapeDtypeStruct((384, 768), BF16),
        in_specs=[VMEM, VMEM],
        out_specs=VMEM,
        compiler_params=pltpu.CompilerParams(vmem_limit_bytes=16 * 2**20),
        cost_estimate=pl.CostEstimate(flops=10**6, bytes_accessed=2 * 10**6, transcendentals=0),
    )(block, tiles)


def copy_rows(part, lat, sems):
    copies = []
    for s in range(3):
        for h in range(2):
            copy = pltpu.make_async_copy(
                part.at[s, pl.ds(288, 96), pl.ds(384 * h, 384)], lat.at[s, pl.ds(96 * h, 96), :], sems.at[s, h]
            )
            copy.start()
            copies.append(copy)
    return copies


def first_kernel(scale, member, field, mine, out, lat, sems):
    for copy in copy_rows(mine, lat, sems):
        copy.wait()
    for s in range(3):
        across = jnp.dot(lat[s], field[...], preferred_element_type=F32)
        out[:, pl.ds(768 * s, 768)] = (scale[s] * member[0] * across).astype(BF16)


def filter_first(scale, member, field, mine):
    return pl.pallas_call(
        first_kernel,
        out_shape=jax.ShapeDtypeStruct((192, 2304), BF16),
        in_specs=[SMEM, SMEM, VMEM, ANY],
        out_specs=VMEM,
        scratch_shapes=[pltpu.VMEM((3, 192, 384), BF16), pltpu.SemaphoreType.DMA((3, 2))],
        compiler_params=pltpu.CompilerParams(vmem_limit_bytes=24 * 2**20),
        cost_estimate=pl.CostEstimate(flops=4 * 10**8, bytes_accessed=2 * 10**6, transcendentals=0),
    )(scale, member, field, mine)


def filter_kernel(core, scale, member, field, first, mine, other, out, lon, lat, mid, lon_sems, lat_sems, sem):
    lat_copies = copy_rows(other, lat, lat_sems)
    rows = pl.ds(pl.multiple_of(core[0] * 192, 64), 192)
    lon_copies = [pltpu.make_async_copy(first, mid.at[rows, :], sem)]
    lon_copies[0].start()
    for s in range(3):
        for m, (part, half) in enumerate(((mine, core[0]), (other, 1 - core[0]))):
            for x in range(4):
                to = pl.ds(pl.multiple_of((2 * x + half) * 96, 32), 96)
                copy = pltpu.make_async_copy(
                    part.at[x, pl.ds(96 * s, 96), :], lon.at[to, pl.ds(768 * s, 768)], lon_sems.at[m, s, x]
                )
                copy.start()
                lon_copies.append(copy)
    for copy in lat_copies:
        copy.wait()
    rows = pl.ds(pl.multiple_of((1 - core[0]) * 192, 64), 192)
    for s in range(3):
        across = jnp.dot(lat[s], field[...], preferred_element_type=F32)
        mid[rows, pl.ds(768 * s, 768)] = (scale[s] * member[0] * across).astype(BF16)
    for copy in lon_copies:
        copy.wait()
    total = lax.dot_general(
        mid[...], lon[...], (((1,), (1,)), ((), ())), preferred_element_type=F32
    )
    out[...] = total.astype(BF16)


def filter_pair(core, scale, member, field, first, mine, other):
    return pl.pallas_call(
        filter_kernel,
        out_shape=jax.ShapeDtypeStruct((384, 768), BF16),
        in_specs=[SMEM, SMEM, SMEM, VMEM, VMEM, ANY, ANY],
        out_specs=VMEM,
        scratch_shapes=[
            pltpu.VMEM((768, 2304), BF16),
            pltpu.VMEM((3, 192, 384), BF16),
            pltpu.VMEM((384, 2304), BF16),
            pltpu.SemaphoreType.DMA((2, 3, 4)),
            pltpu.SemaphoreType.DMA((3, 2)),
            pltpu.SemaphoreType.DMA,
        ],
        compiler_params=pltpu.CompilerParams(vmem_limit_bytes=40 * 2**20),
        cost_estimate=pl.CostEstimate(flops=2 * 10**9, bytes_accessed=5 * 10**6, transcendentals=0),
    )(core, scale, member, field, first, mine, other)


def member_sum(own, back, h, r):
    total = jnp.zeros((8, 768), F32)
    for x in range(4):
        parts = [back[l % 2, x, 4 * h + l // 2, r, :].astype(F32).reshape(1, 768) for l in range(8)]
        total += own[x, r, h].astype(F32) * jnp.concatenate(parts, axis=0)
    return total


def send_kernel(side, own, back, out):
    for r in range(6):
        out[r] = member_sum(own, back, 1 - side[0], r).astype(out.dtype)


def keep_kernel(side, own, back, other, out):
    for r in range(6):
        out[r] = member_sum(own, back, side[0], r) + other[r].astype(F32)


def final_sum(side, own, back):
    common = dict(
        compiler_params=pltpu.CompilerParams(vmem_limit_bytes=16 * 2**20),
        cost_estimate=pl.CostEstimate(flops=10**6, bytes_accessed=10**6, transcendentals=0),
    )
    send = pl.pallas_call(
        send_kernel,
        out_shape=jax.ShapeDtypeStruct((6, 8, 768), BF16),
        in_specs=[SMEM, VMEM, VMEM],
        out_specs=VMEM,
        **common,
    )(side, own, back)
    return pl.pallas_call(
        keep_kernel,
        out_shape=jax.ShapeDtypeStruct((6, 8, 768), F32),
        in_specs=[SMEM, VMEM, VMEM, VMEM],
        out_specs=VMEM,
        **common,
    )(side, own, back, lax.ppermute(send, "zh", SWAP))


def on_device(perturbations, gradient, member_weights, scale_weights, lon_filter, lat_filter):
    x, side, core = lax.axis_index("x"), lax.axis_index("zh"), lax.axis_index("c")
    pairs = [(8 * h + 2 * z + h, 8 * h + 2 * z + h) for h in range(2) for z in range(4)]
    pairs += [(8 * h + 2 * z + 1 - h, 8 * (1 - h) + 2 * (3 - z) + h) for h in range(2) for z in range(4)]
    block = lax.ppermute(lon_filter, ("zh", "zl", "c"), pairs)
    rows = lax.dynamic_index_in_dim(lat_filter, jnp.minimum(x, 2), 0, False)
    tiles = jnp.broadcast_to(jnp.pad(rows, ((0, 2), (0, 0)))[None], (32, 8, 384))
    tiles = lax.all_to_all(tiles, ("zl", "y"), split_axis=0, concat_axis=0, tiled=True)
    packed = pack(block.reshape(288, 768), tiles)
    mine = lax.all_gather(packed, "x", axis=0)

    own = perturbations[0].transpose(1, 0, 2).reshape(6, 4, 2, 8, 768).transpose(1, 0, 2, 3, 4)
    own = lax.all_to_all(own, "x", split_axis=0, concat_axis=0, tiled=True)
    turn = [(4 * a + b, 4 * b + a) for a in range(4) for b in range(4)]
    weight = lax.ppermute(member_weights, ("x", "zl"), turn)
    core, side = core.reshape(1).astype(jnp.int32), side.reshape(1).astype(jnp.int32)
    own, weight, core, side = lax.optimization_barrier((own, weight, core, side))
    level = lax.dynamic_slice_in_dim(gradient.transpose(1, 0, 2), x * 16, 16, axis=1)
    schur = (own.astype(F32) * level.reshape(1, 6, 2, 8, 768)).astype(BF16)
    schur = schur.transpose(0, 2, 3, 1, 4).reshape(64, 2, 2304)
    field = lax.all_to_all(schur, COL, split_axis=0, concat_axis=0, tiled=True).reshape(384, 768)
    mine = lax.optimization_barrier((mine, field))[0]
    other = lax.ppermute(mine, "c", SWAP)
    first = filter_first(scale_weights, weight, field, mine)
    filtered = filter_pair(core, scale_weights, weight, field, first, mine, other).reshape(64, 2, 2304)
    back = lax.all_to_all(filtered, ("c", "zl", "y"), split_axis=0, concat_axis=0, tiled=True)
    total = final_sum(side, own, back.reshape(2, 4, 8, 6, 768))
    return total.transpose(1, 0, 2)


def solution(mesh):
    fine = Mesh(mesh.devices.reshape(4, 2, 4, 8, 2), MEM + COL)
    placed = (
        P(MEM, None, COL, None),
        P(None, COL, None),
        P(MEM),
        P(),
        P(None, MEM, None),
        P(None, COL, None),
    )
    return jax.shard_map(
        on_device, mesh=fine, in_specs=placed, out_specs=P(MEM, COL, None), check_vma=False
    )
```

```python
import jax
import jax.numpy as jnp
from jax import lax
from jax.experimental import pallas as pl
from jax.experimental.pallas import tpu as pltpu
from jax.sharding import Mesh, PartitionSpec as P

MEM = ("x", "zh")
COL = ("zl", "y", "c")
SWAP = [(0, 1), (1, 0)]
F32, BF16 = jnp.float32, jnp.bfloat16


VMEM = pl.BlockSpec(memory_space=pltpu.VMEM)
SMEM = pl.BlockSpec(memory_space=pltpu.SMEM)
ANY = pl.BlockSpec(memory_space=pl.ANY)


def pack_kernel(block, tiles, out):
    out[pl.ds(0, 288), :] = block[...]
    for half in range(2):
        out[pl.ds(288, 96), pl.ds(384 * half, 384)] = tiles[pl.ds(96 * half, 96), :]


def pack(block, tiles):
    return pl.pallas_call(
        pack_kernel,
        out_shape=jax.ShapeDtypeStruct((384, 768), BF16),
        in_specs=[VMEM, VMEM],
        out_specs=VMEM,
        compiler_params=pltpu.CompilerParams(vmem_limit_bytes=16 * 2**20),
        cost_estimate=pl.CostEstimate(flops=10**6, bytes_accessed=2 * 10**6, transcendentals=0),
    )(block, tiles)


def copy_rows(part, lat, sems):
    copies = []
    for s in range(3):
        for h in range(2):
            copy = pltpu.make_async_copy(
                part.at[s, pl.ds(288, 96), pl.ds(384 * h, 384)], lat.at[s, pl.ds(96 * h, 96), :], sems.at[s, h]
            )
            copy.start()
            copies.append(copy)
    return copies


def first_kernel(scale, member, field, mine, out, lat, sems):
    for copy in copy_rows(mine, lat, sems):
        copy.wait()
    for s in range(3):
        across = jnp.dot(lat[s], field[...], preferred_element_type=F32)
        out[:, pl.ds(768 * s, 768)] = (scale[s] * member[0] * across).astype(BF16)


def filter_first(scale, member, field, mine):
    return pl.pallas_call(
        first_kernel,
        out_shape=jax.ShapeDtypeStruct((192, 2304), BF16),
        in_specs=[SMEM, SMEM, VMEM, ANY],
        out_specs=VMEM,
        scratch_shapes=[pltpu.VMEM((3, 192, 384), BF16), pltpu.SemaphoreType.DMA((3, 2))],
        compiler_params=pltpu.CompilerParams(vmem_limit_bytes=24 * 2**20),
        cost_estimate=pl.CostEstimate(flops=4 * 10**8, bytes_accessed=2 * 10**6, transcendentals=0),
    )(scale, member, field, mine)


def filter_kernel(core, scale, member, field, first, mine, other, out, lon, lat, mid, lon_sems, lat_sems, sem):
    lat_copies = copy_rows(other, lat, lat_sems)
    rows = pl.ds(pl.multiple_of(core[0] * 192, 64), 192)
    lon_copies = [pltpu.make_async_copy(first, mid.at[rows, :], sem)]
    lon_copies[0].start()
    for s in range(3):
        for m, (part, half) in enumerate(((mine, core[0]), (other, 1 - core[0]))):
            for x in range(4):
                to = pl.ds(pl.multiple_of((2 * x + half) * 96, 32), 96)
                copy = pltpu.make_async_copy(
                    part.at[x, pl.ds(96 * s, 96), :], lon.at[to, pl.ds(768 * s, 768)], lon_sems.at[m, s, x]
                )
                copy.start()
                lon_copies.append(copy)
    for copy in lat_copies:
        copy.wait()
    rows = pl.ds(pl.multiple_of((1 - core[0]) * 192, 64), 192)
    for s in range(3):
        across = jnp.dot(lat[s], field[...], preferred_element_type=F32)
        mid[rows, pl.ds(768 * s, 768)] = (scale[s] * member[0] * across).astype(BF16)
    for copy in lon_copies:
        copy.wait()
    total = lax.dot_general(
        mid[...], lon[...], (((1,), (1,)), ((), ())), preferred_element_type=F32
    )
    out[...] = total.astype(BF16)


def filter_pair(core, scale, member, field, first, mine, other):
    return pl.pallas_call(
        filter_kernel,
        out_shape=jax.ShapeDtypeStruct((384, 768), BF16),
        in_specs=[SMEM, SMEM, SMEM, VMEM, VMEM, ANY, ANY],
        out_specs=VMEM,
        scratch_shapes=[
            pltpu.VMEM((768, 2304), BF16),
            pltpu.VMEM((3, 192, 384), BF16),
            pltpu.VMEM((384, 2304), BF16),
            pltpu.SemaphoreType.DMA((2, 3, 4)),
            pltpu.SemaphoreType.DMA((3, 2)),
            pltpu.SemaphoreType.DMA,
        ],
        compiler_params=pltpu.CompilerParams(vmem_limit_bytes=40 * 2**20),
        cost_estimate=pl.CostEstimate(flops=2 * 10**9, bytes_accessed=5 * 10**6, transcendentals=0),
    )(core, scale, member, field, first, mine, other)


def member_sum(own, back, h, r):
    total = jnp.zeros((8, 768), F32)
    for x in range(4):
        parts = [back[l % 2, x, 4 * h + l // 2, r, :].astype(F32).reshape(1, 768) for l in range(8)]
        total += own[x, r, h].astype(F32) * jnp.concatenate(parts, axis=0)
    return total


def send_kernel(side, own, back, out):
    for r in range(6):
        out[r] = member_sum(own, back, 1 - side[0], r).astype(out.dtype)


def keep_kernel(side, own, back, other, out):
    for r in range(6):
        out[r] = member_sum(own, back, side[0], r) + other[r].astype(F32)


def final_sum(side, own, back):
    common = dict(
        compiler_params=pltpu.CompilerParams(vmem_limit_bytes=16 * 2**20),
        cost_estimate=pl.CostEstimate(flops=10**6, bytes_accessed=10**6, transcendentals=0),
    )
    send = pl.pallas_call(
        send_kernel,
        out_shape=jax.ShapeDtypeStruct((6, 8, 768), BF16),
        in_specs=[SMEM, VMEM, VMEM],
        out_specs=VMEM,
        **common,
    )(side, own, back)
    return pl.pallas_call(
        keep_kernel,
        out_shape=jax.ShapeDtypeStruct((6, 8, 768), F32),
        in_specs=[SMEM, VMEM, VMEM, VMEM],
        out_specs=VMEM,
        **common,
    )(side, own, back, lax.ppermute(send, "zh", SWAP))


def on_device(perturbations, gradient, member_weights, scale_weights, lon_filter, lat_filter):
    x, side, core = lax.axis_index("x"), lax.axis_index("zh"), lax.axis_index("c")
    pairs = [(8 * h + 2 * z + h, 8 * h + 2 * z + h) for h in range(2) for z in range(4)]
    pairs += [(8 * h + 2 * z + 1 - h, 8 * (1 - h) + 2 * (3 - z) + h) for h in range(2) for z in range(4)]
    block = lax.ppermute(lon_filter, ("zh", "zl", "c"), pairs)
    rows = lax.dynamic_index_in_dim(lat_filter, jnp.minimum(x, 2), 0, False)
    tiles = jnp.broadcast_to(rows.reshape(1, 2, 1152), (32, 2, 1152))
    tiles = lax.all_to_all(tiles, ("zl", "y"), split_axis=0, concat_axis=0, tiled=True).reshape(192, 384)
    packed = pack(block.reshape(288, 768), tiles)
    mine = lax.all_gather(packed, "x", axis=0)

    own = perturbations[0].transpose(1, 0, 2).reshape(6, 4, 2, 8, 768).transpose(1, 0, 2, 3, 4)
    own = lax.all_to_all(own, "x", split_axis=0, concat_axis=0, tiled=True)
    turn = [(4 * a + b, 4 * b + a) for a in range(4) for b in range(4)]
    weight = lax.ppermute(member_weights, ("x", "zl"), turn)
    core, side = core.reshape(1).astype(jnp.int32), side.reshape(1).astype(jnp.int32)
    own, weight, core, side = lax.optimization_barrier((own, weight, core, side))
    level = lax.dynamic_slice_in_dim(gradient.transpose(1, 0, 2), x * 16, 16, axis=1)
    schur = (own.astype(F32) * level.reshape(1, 6, 2, 8, 768)).astype(BF16)
    schur = schur.transpose(0, 2, 3, 1, 4).reshape(64, 2, 2304)
    field = lax.all_to_all(schur, COL, split_axis=0, concat_axis=0, tiled=True).reshape(384, 768)
    mine = lax.optimization_barrier((mine, field))[0]
    other = lax.ppermute(mine, "c", SWAP)
    first = filter_first(scale_weights, weight, field, mine)
    filtered = filter_pair(core, scale_weights, weight, field, first, mine, other).reshape(64, 2, 2304)
    back = lax.all_to_all(filtered, ("c", "zl", "y"), split_axis=0, concat_axis=0, tiled=True)
    total = final_sum(side, own, back.reshape(2, 4, 8, 6, 768))
    return total.transpose(1, 0, 2)


def solution(mesh):
    fine = Mesh(mesh.devices.reshape(4, 2, 4, 8, 2), MEM + COL)
    placed = (
        P(MEM, None, COL, None),
        P(None, COL, None),
        P(MEM),
        P(),
        P(None, MEM, None),
        P(None, COL, None),
    )
    return jax.shard_map(
        on_device, mesh=fine, in_specs=placed, out_specs=P(MEM, COL, None), check_vma=False
    )
```

```python
import jax
import jax.numpy as jnp
from jax import lax
from jax.experimental import pallas as pl
from jax.experimental.pallas import tpu as pltpu
from jax.sharding import Mesh, PartitionSpec as P

MEM = ("x", "zh")
COL = ("zl", "y", "c")
SWAP = [(0, 1), (1, 0)]
F32, BF16 = jnp.float32, jnp.bfloat16


VMEM = pl.BlockSpec(memory_space=pltpu.VMEM)
SMEM = pl.BlockSpec(memory_space=pltpu.SMEM)
ANY = pl.BlockSpec(memory_space=pl.ANY)


def pack_kernel(block, tiles, out):
    out[pl.ds(0, 288), :] = block[...]
    for half in range(2):
        out[pl.ds(288, 96), pl.ds(384 * half, 384)] = tiles[pl.ds(96 * half, 96), :]


def pack(block, tiles):
    return pl.pallas_call(
        pack_kernel,
        out_shape=jax.ShapeDtypeStruct((384, 768), BF16),
        in_specs=[VMEM, VMEM],
        out_specs=VMEM,
        compiler_params=pltpu.CompilerParams(vmem_limit_bytes=16 * 2**20),
        cost_estimate=pl.CostEstimate(flops=10**6, bytes_accessed=2 * 10**6, transcendentals=0),
    )(block, tiles)


def copy_rows(part, lat, sems):
    copies = []
    for s in range(3):
        for h in range(2):
            copy = pltpu.make_async_copy(
                part.at[s, pl.ds(288, 96), pl.ds(384 * h, 384)], lat.at[s, pl.ds(96 * h, 96), :], sems.at[s, h]
            )
            copy.start()
            copies.append(copy)
    return copies


def first_kernel(scale, member, field, mine, out, lat, sems):
    for copy in copy_rows(mine, lat, sems):
        copy.wait()
    for s in range(3):
        across = jnp.dot(lat[s], field[...], preferred_element_type=F32)
        out[:, pl.ds(768 * s, 768)] = (scale[s] * member[0] * across).astype(BF16)


def filter_first(scale, member, field, mine):
    return pl.pallas_call(
        first_kernel,
        out_shape=jax.ShapeDtypeStruct((192, 2304), BF16),
        in_specs=[SMEM, SMEM, VMEM, ANY],
        out_specs=VMEM,
        scratch_shapes=[pltpu.VMEM((3, 192, 384), BF16), pltpu.SemaphoreType.DMA((3, 2))],
        compiler_params=pltpu.CompilerParams(vmem_limit_bytes=24 * 2**20),
        cost_estimate=pl.CostEstimate(flops=4 * 10**8, bytes_accessed=2 * 10**6, transcendentals=0),
    )(scale, member, field, mine)


def filter_kernel(core, scale, member, field, first, mine, other, out, lon, lat, mid, lon_sems, lat_sems, sem):
    lat_copies = copy_rows(other, lat, lat_sems)
    rows = pl.ds(pl.multiple_of(core[0] * 192, 64), 192)
    lon_copies = [pltpu.make_async_copy(first, mid.at[rows, :], sem)]
    lon_copies[0].start()
    for s in range(3):
        for m, (part, half) in enumerate(((mine, core[0]), (other, 1 - core[0]))):
            for x in range(4):
                to = pl.ds(pl.multiple_of((2 * x + half) * 96, 32), 96)
                copy = pltpu.make_async_copy(
                    part.at[x, pl.ds(96 * s, 96), :], lon.at[to, pl.ds(768 * s, 768)], lon_sems.at[m, s, x]
                )
                copy.start()
                lon_copies.append(copy)
    for copy in lat_copies:
        copy.wait()
    rows = pl.ds(pl.multiple_of((1 - core[0]) * 192, 64), 192)
    for s in range(3):
        across = jnp.dot(lat[s], field[...], preferred_element_type=F32)
        mid[rows, pl.ds(768 * s, 768)] = (scale[s] * member[0] * across).astype(BF16)
    for copy in lon_copies:
        copy.wait()
    total = lax.dot_general(
        mid[...], lon[...], (((1,), (1,)), ((), ())), preferred_element_type=F32
    )
    out[...] = total.astype(BF16)


def filter_pair(core, scale, member, field, first, mine, other):
    return pl.pallas_call(
        filter_kernel,
        out_shape=jax.ShapeDtypeStruct((384, 768), BF16),
        in_specs=[SMEM, SMEM, SMEM, VMEM, VMEM, ANY, ANY],
        out_specs=VMEM,
        scratch_shapes=[
            pltpu.VMEM((768, 2304), BF16),
            pltpu.VMEM((3, 192, 384), BF16),
            pltpu.VMEM((384, 2304), BF16),
            pltpu.SemaphoreType.DMA((2, 3, 4)),
            pltpu.SemaphoreType.DMA((3, 2)),
            pltpu.SemaphoreType.DMA,
        ],
        compiler_params=pltpu.CompilerParams(vmem_limit_bytes=40 * 2**20),
        cost_estimate=pl.CostEstimate(flops=2 * 10**9, bytes_accessed=5 * 10**6, transcendentals=0),
    )(core, scale, member, field, first, mine, other)


def member_sum(own, back, h, r):
    total = jnp.zeros((8, 768), F32)
    for x in range(4):
        parts = [back[l % 2, x, 4 * h + l // 2, r, :].astype(F32).reshape(1, 768) for l in range(8)]
        total += own[x, r, h].astype(F32) * jnp.concatenate(parts, axis=0)
    return total


def send_kernel(side, own, back, out):
    for r in range(6):
        out[r] = member_sum(own, back, 1 - side[0], r).astype(out.dtype)


def keep_kernel(side, own, back, other, out):
    for r in range(6):
        out[r] = member_sum(own, back, side[0], r) + other[r].astype(F32)


def final_sum(side, own, back):
    common = dict(
        compiler_params=pltpu.CompilerParams(vmem_limit_bytes=16 * 2**20),
        cost_estimate=pl.CostEstimate(flops=10**6, bytes_accessed=10**6, transcendentals=0),
    )
    send = pl.pallas_call(
        send_kernel,
        out_shape=jax.ShapeDtypeStruct((6, 8, 768), BF16),
        in_specs=[SMEM, VMEM, VMEM],
        out_specs=VMEM,
        **common,
    )(side, own, back)
    return pl.pallas_call(
        keep_kernel,
        out_shape=jax.ShapeDtypeStruct((6, 8, 768), F32),
        in_specs=[SMEM, VMEM, VMEM, VMEM],
        out_specs=VMEM,
        **common,
    )(side, own, back, lax.ppermute(send, "zh", SWAP))


def on_device(perturbations, gradient, member_weights, scale_weights, lon_filter, lat_filter):
    x, side, core = lax.axis_index("x"), lax.axis_index("zh"), lax.axis_index("c")
    pairs = [(8 * h + 2 * z + h, 8 * h + 2 * z + h) for h in range(2) for z in range(4)]
    pairs += [(8 * h + 2 * z + 1 - h, 8 * (1 - h) + 2 * (3 - z) + h) for h in range(2) for z in range(4)]
    block = lax.ppermute(lon_filter, ("zh", "zl", "c"), pairs)
    rows = lax.dynamic_index_in_dim(lat_filter, jnp.minimum(x, 2), 0, False)
    tiles = jnp.broadcast_to(rows.reshape(1, 2, 1152), (32, 2, 1152))
    tiles = lax.all_to_all(tiles, ("zl", "y"), split_axis=0, concat_axis=0, tiled=True).reshape(192, 384)
    own = perturbations[0].transpose(1, 0, 2).reshape(6, 4, 2, 8, 768).transpose(1, 0, 2, 3, 4)
    own, block = lax.optimization_barrier((own, block))
    packed = pack(block.reshape(288, 768), tiles)
    mine = lax.all_gather(packed, "x", axis=0)

    own = lax.all_to_all(own, "x", split_axis=0, concat_axis=0, tiled=True)
    turn = [(4 * a + b, 4 * b + a) for a in range(4) for b in range(4)]
    weight = lax.ppermute(member_weights, ("x", "zl"), turn)
    core, side = core.reshape(1).astype(jnp.int32), side.reshape(1).astype(jnp.int32)
    own, weight, core, side = lax.optimization_barrier((own, weight, core, side))
    level = lax.dynamic_slice_in_dim(gradient.transpose(1, 0, 2), x * 16, 16, axis=1)
    schur = (own.astype(F32) * level.reshape(1, 6, 2, 8, 768)).astype(BF16)
    schur = schur.transpose(0, 2, 3, 1, 4).reshape(64, 2, 2304)
    field = lax.all_to_all(schur, COL, split_axis=0, concat_axis=0, tiled=True).reshape(384, 768)
    mine = lax.optimization_barrier((mine, field))[0]
    other = lax.ppermute(mine, "c", SWAP)
    first = filter_first(scale_weights, weight, field, mine)
    filtered = filter_pair(core, scale_weights, weight, field, first, mine, other).reshape(64, 2, 2304)
    back = lax.all_to_all(filtered, ("c", "zl", "y"), split_axis=0, concat_axis=0, tiled=True)
    total = final_sum(side, own, back.reshape(2, 4, 8, 6, 768))
    return total.transpose(1, 0, 2)


def solution(mesh):
    fine = Mesh(mesh.devices.reshape(4, 2, 4, 8, 2), MEM + COL)
    placed = (
        P(MEM, None, COL, None),
        P(None, COL, None),
        P(MEM),
        P(),
        P(None, MEM, None),
        P(None, COL, None),
    )
    return jax.shard_map(
        on_device, mesh=fine, in_specs=placed, out_specs=P(MEM, COL, None), check_vma=False
    )
```
